128 devices in a mesh: dp: 64 (over z, y, x), tensor: 2 (over core).
Axes of the slice: x: 4, y: 4, z: 4, core: 2. Of those that a mesh axis runs over, the one named last changes fastest.
Arguments:
- acts: bfloat16 [32768, 8192], P(('dp', 'tensor')), may hold values from -6 to 6
- out_grad: bfloat16 [32768, 1024], P('dp', 'tensor'), may hold values from -6 to 6
- weight: bfloat16 [8192, 1024], P(None, 'tensor'), may hold values from -0.0625 to 0.0625
- error: bfloat16 [524288, 1024], P('dp', 'tensor'), may hold values from -4 to 4
- momentum: bfloat16 [8192, 1024], P('dp', 'tensor'), may hold values from -2 to 2
- q_init: float32 [1024, 32], P('tensor'), may hold values from -6 to 6
Outputs:
- new_error: bfloat16 [524288, 1024], P('dp', 'tensor')
- new_momentum: bfloat16 [8192, 1024], P('dp', 'tensor')
- input_grad: bfloat16 [32768, 8192], P(('dp', 'tensor'))
The draws below stay inside these ranges and needn't reach their ends.
All inputs are finite; a program needn't handle non-finite values.
Results may differ from the reference program's by a relative error of at most 0.01.
Values may be sent and summed in bfloat16 or wider, within the bound.
No kernel may reach another device: no remote copies, remote signals or barrier semaphores. Data moves between devices by JAX's collectives and lax.ppermute only.
A program may use at most 192 MiB of HBM per device.

```python
import jax
import jax.numpy as jnp
from jax import lax

D = 8192
RANK = 32
TOKENS = 512
KV = 1024
COLS = 512
REPLICAS = 64
N_TENSOR = 2


def steps_of(stream_key, extent, pieces, least, high):
    gain = 1.0
    for position, parts in pieces:
        steps = jax.random.uniform(jax.random.fold_in(jax.random.fold_in(stream_key, 6), position), (parts,), jnp.float32, least / len(pieces), high / len(pieces))
        gain = gain * jnp.repeat(jnp.exp(steps), extent[position] // parts).reshape((-1,) + (1,) * (len(extent) - 1 - position))
    return gain


def gaussian(stream_key, extent, scale, most, split=(), kind=jnp.bfloat16):
    values = scale * jax.random.normal(stream_key, extent, jnp.float32)
    if split:
        values = values * steps_of(stream_key, extent, split, -0.22, 0.18)
    return jnp.clip(values, -most, most).astype(kind)


def setup_inputs(seed: int = 0) -> dict:
    splits = jax.random.split(jax.random.key(seed), 7)
    return {
        "acts": gaussian(splits[0], (REPLICAS * TOKENS, D), 1.0, 6.0, ((0, 128),)),
        "out_grad": gaussian(splits[1], (REPLICAS * TOKENS, KV), 1.0, 6.0, ((0, 64), (1, 2))),
        "weight": gaussian(splits[2], (D, KV), D ** -0.5, 0.0625, ((1, 2),)),
        "error": gaussian(splits[3], (REPLICAS * D, KV), 0.5, 4.0, ((0, 64), (1, 2))),
        "momentum": gaussian(splits[4], (D, KV), 0.3, 2.0, ((0, 64), (1, 2))),
        "q_init": gaussian(splits[5], (KV, RANK), 1.0, 6.0, ((0, 2),), jnp.float32),
    }


def orthonormal(block):
    width = block.shape[1]

    def step(k, current):
        column = lax.dynamic_slice_in_dim(current, k, 1, 1)[:, 0]
        keep = (jnp.arange(width) < k).astype(jnp.float32)
        coeff = jnp.dot(column, current, precision=lax.Precision.HIGHEST) * keep
        column = column - jnp.dot(current, coeff, precision=lax.Precision.HIGHEST)
        column = column * lax.rsqrt(jnp.sum(column * column) + 1e-06)
        return lax.dynamic_update_slice_in_dim(current, column[:, None], k, 1)
    return lax.fori_loop(0, width, step, block)

def reference(acts, out_grad, weight, error, momentum, q_init):
    scale = 1.0 / TOKENS ** 0.5
    acts_r = acts.reshape(REPLICAS, TOKENS, D)
    grads_r = out_grad.reshape(REPLICAS, TOKENS, KV)
    error_r = error.reshape(REPLICAS, D, KV)

    def merge_one(inputs):
        rows, grads, old = inputs
        grad = jnp.dot(rows.T, grads, preferred_element_type=jnp.float32)
        return grad * scale + old.astype(jnp.float32)
    merged = lax.map(merge_one, (acts_r, grads_r, error_r))
    blocks = merged.reshape(REPLICAS, D, N_TENSOR, COLS)
    q_blocks = q_init.reshape(N_TENSOR, COLS, RANK)
    left = jnp.einsum('rdbc,bck->bdk', blocks, q_blocks, precision=lax.Precision.HIGHEST)
    basis = jax.vmap(orthonormal)(left)
    right = jnp.einsum('rdbc,bdk->bck', blocks, basis, precision=lax.Precision.HIGHEST) / REPLICAS
    approx = jnp.einsum('bdk,bck->dbc', basis, right, precision=lax.Precision.HIGHEST).reshape(D, KV)
    new_error = (merged - approx[None]).astype(jnp.bfloat16).reshape(REPLICAS * D, KV)
    new_momentum = (0.9 * momentum.astype(jnp.float32) + approx).astype(jnp.bfloat16)

    def input_one(grads):
        total = jnp.zeros((TOKENS, D), jnp.float32)
        for block_id in range(N_TENSOR):
            lo = block_id * COLS
            part = jnp.dot(grads[:, lo:lo + COLS], weight[:, lo:lo + COLS].T, preferred_element_type=jnp.float32)
            total = total + lax.optimization_barrier(part.astype(jnp.bfloat16)).astype(jnp.float32)
        return total.astype(jnp.bfloat16)
    input_grad = lax.map(input_one, grads_r).reshape(REPLICAS * TOKENS, D)
    return (new_error, new_momentum, input_grad)
```

```python
import functools

import jax
import jax.numpy as jnp
from jax import lax
from jax.experimental import pallas as pl
from jax.experimental.pallas import tpu as pltpu
from jax.sharding import PartitionSpec as P

F32 = jnp.float32
BF16 = jnp.bfloat16
MIB = 1024 * 1024
BLOCK = 512
CHUNK = 128
GROUP = 8

NT = (((1,), (1,)), ((), ()))
TN = (((0,), (0,)), ((), ()))


def dot(a, b, dims=(((1,), (0,)), ((), ()))):
    return lax.dot_general(a, b, dims, preferred_element_type=F32)


def split3(x):
    high = x.astype(BF16)
    rest = x - high.astype(F32)
    middle = rest.astype(BF16)
    low = (rest - middle.astype(F32)).astype(BF16)
    return jnp.concatenate([high, middle, low], axis=0)


def sum3(x):
    rows = x.shape[0] // 3
    return x[:rows] + x[rows : 2 * rows] + x[2 * rows :]


def call(kernel, place, grid, in_specs, out_specs, out_shape, args, flops, moved, scratch=(), vmem=48):
    return pl.pallas_call(
        kernel,
        grid_spec=pltpu.PrefetchScalarGridSpec(
            num_scalar_prefetch=1,
            grid=grid,
            in_specs=in_specs,
            out_specs=out_specs,
            scratch_shapes=list(scratch),
        ),
        out_shape=out_shape,
        compiler_params=pltpu.CompilerParams(vmem_limit_bytes=vmem * MIB),
        cost_estimate=pl.CostEstimate(flops=flops, bytes_accessed=moved, transcendentals=0),
    )(place, *args)


def whole(*shape):
    return pl.BlockSpec(shape, lambda *_: (0,) * len(shape))


def left_own_kernel(scale, place, q_ref, og_own, og_oth, acts, error, part, pq_oth, q3, pq3):
    @pl.when(pl.program_id(0) == 0)
    def _():
        q3[...] = split3(q_ref[...])
        pq3[...] = split3(sum3(dot(q3[...], og_own[...], NT)) * scale)
        pq_oth[...] = split3(sum3(dot(q3[...], og_oth[...], NT)) * scale)

    part[...] = sum3(dot(q3[...], error[...], NT)) + sum3(dot(pq3[...], acts[...]))


def left_kernel(place, pq3, acts, part, left):
    total = part[...] + sum3(dot(pq3[...], acts[...]))
    for i in range(left.shape[0]):
        left[i] = total[:, i * CHUNK : (i + 1) * CHUNK].astype(BF16)


def input_kernel(place, og_own, og_oth, weight, own, oth):
    own[...] = dot(og_own[...], weight[...], NT).astype(BF16)
    oth[...] = dot(og_oth[...], weight[...], NT).astype(BF16)


def merged_kernel(scale, place, og_own, og_oth, acts_own, acts_oth, error, merged):
    grad = dot(acts_own[...], og_own[...], TN) + dot(acts_oth[...], og_oth[...], TN)
    merged[...] = grad * scale + error[...].astype(F32)


def add_kernel(place, own, other, out):
    out[...] = (own[...].astype(F32) + other[...].astype(F32)).astype(BF16)


def left_sum_kernel(place, parts, out):
    total = jnp.sum(parts[...].astype(F32), axis=0).astype(BF16)
    out[...] = jnp.broadcast_to(total[None], out.shape)


def join(left):
    return jnp.concatenate([left[i] for i in range(left.shape[0])], axis=1)


def right_kernel(scale, place, og_own, og_oth, left, acts_own, acts_oth, error, right, gram, r_acc, own_acc, oth_acc):
    step = pl.program_id(0)

    @pl.when(step == 0)
    def _():
        r_acc[...] = jnp.zeros_like(r_acc)
        own_acc[...] = jnp.zeros_like(own_acc)
        oth_acc[...] = jnp.zeros_like(oth_acc)
        gram[...] = jnp.zeros_like(gram)

    block = join(left)
    r_acc[...] += dot(block, error[...])
    own_acc[...] += dot(block, acts_own[...], NT)
    oth_acc[...] += dot(block, acts_oth[...], NT)
    gram[...] += dot(block, block, NT)

    @pl.when(step == pl.num_programs(0) - 1)
    def _():
        total = r_acc[...]
        total += sum3(dot(split3(own_acc[...] * scale), og_own[...]))
        total += sum3(dot(split3(oth_acc[...] * scale), og_oth[...]))
        for i in range(right.shape[0]):
            right[i] = total


def gram_schmidt_kernel(place, gram, out):
    width = gram.shape[0]
    g = gram[...]
    rows = lax.broadcasted_iota(jnp.int32, (width, width), 0)
    columns = lax.broadcasted_iota(jnp.int32, (width, width), 1)
    coeffs = jnp.zeros((width, width), F32)
    products = jnp.zeros((width, width), F32)
    for k in range(width):
        along = jnp.sum(jnp.where(columns == k, products, 0.0), axis=1, keepdims=True)
        unit = (columns[:1] == k).astype(F32)
        v = unit - jnp.sum(along * coeffs, axis=0, keepdims=True)
        inner = g[k : k + 1] - jnp.sum(along * products, axis=0, keepdims=True)
        square = jnp.maximum(jnp.sum(v * inner, axis=1, keepdims=True), 0.0)
        inverse = lax.rsqrt(square + 1e-06)
        coeffs = jnp.where(rows == k, v * inverse, coeffs)
        products = jnp.where(rows == k, inner * inverse, products)
    out[...] = lax.dot_general(
        coeffs, coeffs, TN, precision=lax.Precision.HIGHEST, preferred_element_type=F32
    )


def right_sum_kernel(place, parts, out):
    total = jnp.sum(parts[...], axis=0)
    out[...] = jnp.broadcast_to(total[None], out.shape)


def final_kernel(inverse_replicas, place, parts, metric, left_mine, momentum, left, merged, new_error, new_momentum, w3):
    @pl.when(pl.program_id(0) == 0)
    def _():
        total = jnp.sum(parts[...], axis=0) * inverse_replicas
        w3[...] = split3(
            jnp.dot(metric[...], total, precision=lax.Precision.HIGHEST, preferred_element_type=F32)
        )
        mine = jnp.concatenate([left_mine[0]] * 3, axis=0)
        approx = dot(mine, w3[...], TN)
        new_momentum[...] = (0.9 * momentum[...].astype(F32) + approx).astype(BF16)

    block = jnp.concatenate([join(left)] * 3, axis=0)
    new_error[...] = (merged[...] - dot(block, w3[...], TN)).astype(BF16)


def per_device(acts, out_grad, weight, error, momentum, q_init):
    tokens, cols = out_grad.shape
    half, width = acts.shape
    rank = q_init.shape[1]
    replicas = lax.axis_size("dp")
    scale = 1.0 / tokens**0.5
    steps = width // BLOCK
    per_step = BLOCK // CHUNK
    core = lax.axis_index("tensor")
    place = jnp.stack([core, 1 - core, lax.axis_index("dp")]).astype(jnp.int32)
    swap = [(0, 1), (1, 0)]
    shape = jax.ShapeDtypeStruct

    og_own = pl.BlockSpec((half, cols), lambda i, p: (p[0], 0))
    og_oth = pl.BlockSpec((half, cols), lambda i, p: (p[1], 0))
    over_lanes = lambda rows: pl.BlockSpec((rows, BLOCK), lambda i, p: (0, i))
    over_rows = pl.BlockSpec((BLOCK, cols), lambda i, p: (i, 0))
    chunks = pl.BlockSpec((per_step, rank, CHUNK), lambda i, p: (i, 0, 0))

    acts_oth = lax.ppermute(acts, "tensor", swap)

    part, pq_oth = call(
        functools.partial(left_own_kernel, scale),
        place,
        (steps,),
        [whole(rank, cols), og_own, og_oth, over_lanes(half), over_rows],
        [over_lanes(rank), whole(3 * rank, half)],
        [shape((rank, width), F32), shape((3 * rank, half), BF16)],
        (q_init.T, out_grad, out_grad, acts, error),
        flops=2 * 96 * width * 768,
        moved=13 * MIB,
        scratch=[pltpu.VMEM((3 * rank, cols), BF16), pltpu.VMEM((3 * rank, half), BF16)],
    )
    left_parts = call(
        left_kernel,
        place,
        (steps,),
        [whole(3 * rank, half), over_lanes(half), over_lanes(rank)],
        chunks,
        shape((replicas, rank, CHUNK), BF16),
        (pq_oth, acts_oth, part),
        flops=2 * 96 * width * 256,
        moved=6 * MIB,
    )
    gathered = lax.all_to_all(left_parts, "dp", 0, 0, tiled=True)

    own_input, oth_input = call(
        input_kernel,
        place,
        (steps,),
        [og_own, og_oth, over_rows],
        [over_lanes(half)] * 2,
        [shape((half, width), BF16)] * 2,
        (out_grad, out_grad, weight),
        flops=2 * tokens * cols * width,
        moved=17 * MIB,
    )
    received = lax.ppermute(oth_input, "tensor", swap)
    merged = call(
        functools.partial(merged_kernel, scale),
        place,
        (steps,),
        [og_own, og_oth, over_lanes(half), over_lanes(half), over_rows],
        over_rows,
        shape((width, cols), F32),
        (out_grad, out_grad, acts, acts_oth, error),
        flops=2 * tokens * cols * width,
        moved=33 * MIB,
    )

    left_copies = call(
        left_sum_kernel,
        place,
        (1,),
        [whole(replicas, rank, CHUNK)],
        whole(replicas, rank, CHUNK),
        shape((replicas, rank, CHUNK), BF16),
        (gathered,),
        flops=replicas * rank * CHUNK,
        moved=MIB,
    )
    left = lax.all_to_all(left_copies, "dp", 0, 0, tiled=True)
    input_grad = call(
        add_kernel,
        place,
        (8,),
        [pl.BlockSpec((half // 8, width), lambda i, p: (i, 0))] * 2,
        pl.BlockSpec((half // 8, width), lambda i, p: (i, 0)),
        shape((half, width), BF16),
        (own_input, received),
        flops=half * width,
        moved=12 * MIB,
    )

    right_copies, gram = call(
        functools.partial(right_kernel, scale),
        place,
        (steps,),
        [og_own, og_oth, chunks, over_lanes(half), over_lanes(half), over_rows],
        [whole(GROUP, rank, cols), whole(rank, rank)],
        [shape((GROUP, rank, cols), F32), shape((rank, rank), F32)],
        (out_grad, out_grad, left, acts, acts_oth, error),
        flops=2 * rank * width * 1024,
        moved=17 * MIB,
        scratch=[pltpu.VMEM((rank, cols), F32), pltpu.VMEM((rank, half), F32), pltpu.VMEM((rank, half), F32)],
    )
    metric = call(
        gram_schmidt_kernel,
        place,
        (1,),
        [whole(rank, rank)],
        whole(rank, rank),
        shape((rank, rank), F32),
        (gram,),
        flops=rank**3,
        moved=8192,
    )
    near = [[g * GROUP + i for i in range(GROUP)] for g in range(replicas // GROUP)]
    far = [[i * (replicas // GROUP) + g for i in range(GROUP)] for g in range(replicas // GROUP)]
    first = lax.all_to_all(right_copies, "dp", 0, 0, tiled=True, axis_index_groups=near)
    second_copies = call(
        right_sum_kernel,
        place,
        (1,),
        [whole(GROUP, rank, cols)],
        whole(GROUP, rank, cols),
        shape((GROUP, rank, cols), F32),
        (first,),
        flops=GROUP * rank * cols,
        moved=MIB,
    )
    second = lax.all_to_all(second_copies, "dp", 0, 0, tiled=True, axis_index_groups=far)
    new_error, new_momentum = call(
        functools.partial(final_kernel, 1.0 / replicas),
        place,
        (steps,),
        [
            whole(GROUP, rank, cols),
            whole(rank, rank),
            pl.BlockSpec((1, rank, CHUNK), lambda i, p: (p[2], 0, 0)),
            whole(CHUNK, cols),
            chunks,
            over_rows,
        ],
        [over_rows, whole(CHUNK, cols)],
        [shape((width, cols), BF16), shape((CHUNK, cols), BF16)],
        (second, metric, left, momentum, left, merged),
        flops=2 * 96 * width * cols,
        moved=25 * MIB,
        scratch=[pltpu.VMEM((3 * rank, cols), BF16)],
    )
    return (new_error, new_momentum, input_grad)


def solution(mesh):
    return jax.shard_map(
        per_device,
        mesh=mesh,
        in_specs=(
            P(("dp", "tensor"), None),
            P("dp", "tensor"),
            P(None, "tensor"),
            P("dp", "tensor"),
            P("dp", "tensor"),
            P("tensor", None),
        ),
        out_specs=(P("dp", "tensor"), P("dp", "tensor"), P(("dp", "tensor"), None)),
        check_vma=False,
    )
```

```python
import functools

import jax
import jax.numpy as jnp
from jax import lax
from jax.experimental import pallas as pl
from jax.experimental.pallas import tpu as pltpu
from jax.sharding import PartitionSpec as P

F32 = jnp.float32
BF16 = jnp.bfloat16
MIB = 1024 * 1024
BLOCK = 1024
CHUNK = 128
GROUP = 8

NN = (((1,), (0,)), ((), ()))
NT = (((1,), (1,)), ((), ()))
TN = (((0,), (0,)), ((), ()))

VMEM = pl.BlockSpec(memory_space=pltpu.VMEM)
SMEM = pl.BlockSpec(memory_space=pltpu.SMEM)
HBM = pl.BlockSpec(memory_space=pltpu.HBM)
TOKEN = jax.ShapeDtypeStruct((8, 128), jnp.float32)


def in_hbm(x):
    return pltpu.with_memory_space_constraint(x, pltpu.HBM)


def dot(a, b, dims=NN):
    return lax.dot_general(a, b, dims, preferred_element_type=F32)


def exact_dot(a, b, dims=NN):
    return lax.dot_general(a, b, dims, precision=lax.Precision.HIGHEST, preferred_element_type=F32)


def split3(x, axis=0):
    high = x.astype(BF16)
    rest = x - high.astype(F32)
    middle = rest.astype(BF16)
    low = (rest - middle.astype(F32)).astype(BF16)
    return jnp.concatenate([high, middle, low], axis=axis)


def sum3(x):
    rows = x.shape[0] // 3
    return x[:rows] + x[rows : 2 * rows] + x[2 * rows :]


def call(kernel, in_specs, out_specs, out_shape, args, flops, moved, scratch=(), aliases={}):
    args = [in_hbm(x) if spec is HBM else x for spec, x in zip(in_specs, args)]
    return pl.pallas_call(
        kernel,
        in_specs=in_specs,
        out_specs=out_specs,
        out_shape=out_shape,
        scratch_shapes=list(scratch),
        input_output_aliases=aliases,
        compiler_params=pltpu.CompilerParams(vmem_limit_bytes=48 * MIB),
        cost_estimate=pl.CostEstimate(flops=flops, bytes_accessed=moved, transcendentals=0),
    )(*args)


def halves(place, og, half):
    own = pl.multiple_of(place[0] * half, half)
    oth = pl.multiple_of(place[1] * half, half)
    return og[pl.ds(own, half), :], og[pl.ds(oth, half), :]


def blocks(width):
    return [slice(i, i + BLOCK) for i in range(0, width, BLOCK)]


class Reader:
    ahead = 3

    def __init__(self, pairs, sems):
        self.copies = [
            [pltpu.make_async_copy(source, target, sems.at[i, j]) for j, (source, target) in enumerate(block)]
            for i, block in enumerate(pairs)
        ]
        for block in self.copies[: self.ahead]:
            for copy in block:
                copy.start()

    def wait(self, i):
        if i + self.ahead < len(self.copies):
            for copy in self.copies[i + self.ahead]:
                copy.start()
        for copy in self.copies[i]:
            copy.wait()


class Writer:
    def __init__(self, slots, sems):
        self.slots, self.sems, self.copies = slots, sems, []

    def put(self, value, target):
        at = len(self.copies)
        slot = at % self.slots.shape[0]
        if at >= self.slots.shape[0]:
            self.copies[at - self.slots.shape[0]].wait()
        self.slots[slot] = value
        copy = pltpu.make_async_copy(self.slots.at[slot], target, self.sems.at[slot])
        copy.start()
        self.copies.append(copy)

    def finish(self):
        for copy in self.copies[-self.slots.shape[0] :]:
            copy.wait()


def left_own_kernel(
    scale, place, q_hbm, og_hbm, acts, error, part, pq_oth, q, og, acts_here, error_here, sems, small_sems
):
    half, width = acts.shape
    rows = blocks(width)
    q_copy = pltpu.make_async_copy(q_hbm, q, small_sems.at[0])
    og_copy = pltpu.make_async_copy(og_hbm, og, small_sems.at[1])
    q_copy.start()
    og_copy.start()
    reader = Reader([[(error.at[at, :], error_here.at[at, :]), (acts.at[:, at], acts_here.at[:, at])] for at in rows], sems)
    q_copy.wait()
    og_copy.wait()
    q3 = split3(q[...])
    og_own, og_oth = halves(place, og, half)
    pq3 = split3(sum3(dot(q3, og_own, NT)) * scale)
    pq_oth[...] = split3(sum3(dot(q3, og_oth, NT)) * scale)
    for i, at in enumerate(rows):
        reader.wait(i)
        by_error = dot(error_here[at, :], q3, NT)
        part[:, at] = sum3(by_error.T) + sum3(dot(pq3, acts_here[:, at]))


def left_kernel(pq3, acts, part, left, token):
    token[...] = jnp.zeros_like(token)
    for at in blocks(acts.shape[1]):
        total = part[:, at] + sum3(dot(pq3[...], acts[:, at]))
        for i in range(BLOCK // CHUNK):
            left[at.start // CHUNK + i] = total[:, i * CHUNK : (i + 1) * CHUNK].astype(BF16)


def merged_kernel(
    scale, place, og, acts, acts_oth, error, after, merged, token,
    acts_here, oth_here, error_here, slots, sems, out_sems,
):
    token[...] = jnp.zeros_like(token)
    half, width = acts.shape
    rows = blocks(width)
    reader = Reader(
        [
            [
                (acts.at[:, at], acts_here.at[:, at]),
                (acts_oth.at[:, at], oth_here.at[:, at]),
                (error.at[at, :], error_here.at[at, :]),
            ]
            for at in rows
        ],
        sems,
    )
    own, oth = halves(place, og, half)
    writer = Writer(slots, out_sems)
    for i, at in enumerate(rows):
        reader.wait(i)
        grad = dot(acts_here[:, at], own, TN) + dot(oth_here[:, at], oth, TN)
        writer.put(grad * scale + error_here[at, :].astype(F32), merged.at[at, :])
    writer.finish()


def input_kernel(place, og, weight, after, own_part, oth_part, token, weight_here, own_slots, oth_slots, sems, own_sems, oth_sems):
    token[...] = jnp.zeros_like(token)
    half, width = own_part.shape
    rows = blocks(width)
    reader = Reader([[(weight.at[at, :], weight_here.at[at, :])] for at in rows], sems)
    own, oth = halves(place, og, half)
    both = jnp.concatenate([own, oth], axis=0)
    own_out = Writer(own_slots, own_sems)
    oth_out = Writer(oth_slots, oth_sems)
    for i, at in enumerate(rows):
        reader.wait(i)
        product = dot(both, weight_here[at, :], NT).astype(BF16)
        oth_out.put(product[half:], oth_part.at[:, at])
        own_out.put(product[:half], own_part.at[:, at])
    own_out.finish()
    oth_out.finish()


def pass_kernel(part, left, after, out, token):
    token[...] = left[0, :8].astype(F32)


def add_kernel(own, other, after, out, token, own_here, other_here, slots, sems, out_sems):
    token[...] = jnp.zeros_like(token)
    rows = blocks(own.shape[1])
    reader = Reader([[(own.at[:, at], own_here.at[:, at]), (other.at[:, at], other_here.at[:, at])] for at in rows], sems)
    writer = Writer(slots, out_sems)
    for i, at in enumerate(rows):
        reader.wait(i)
        writer.put((own_here[:, at].astype(F32) + other_here[:, at].astype(F32)).astype(BF16), out.at[:, at])
    writer.finish()


def left_sum_kernel(parts, after, out, token):
    token[...] = jnp.zeros_like(token)
    total = jnp.sum(parts[...].astype(F32), axis=0).astype(BF16)
    out[...] = jnp.broadcast_to(total[None], out.shape)


def right_kernel(
    scale, place, og, left, acts, acts_oth, error, after, right, gram, left_rows, stack, error_here, sems
):
    tokens, cols = og.shape
    half, width = acts.shape
    rows = blocks(width)
    reader = Reader(
        [
            [
                (acts.at[:, at], stack.at[:half, at]),
                (acts_oth.at[:, at], stack.at[half:tokens, at]),
                (error.at[at, :], error_here.at[at, :]),
            ]
            for at in rows
        ],
        sems,
    )
    for i in range(left.shape[0]):
        stack[tokens:, i * CHUNK : (i + 1) * CHUNK] = left[i]
    left_rows[...] = stack[tokens:, :]
    by_stack, result = None, None
    for i, at in enumerate(rows):
        reader.wait(i)
        here = stack[tokens:, at]
        stack_term = dot(stack[:, at], here, NT)
        error_term = dot(here, error_here[at, :])
        by_stack = stack_term if by_stack is None else by_stack + stack_term
        result = error_term if result is None else result + error_term
    gram[...] = by_stack[tokens:]
    own, oth = halves(place, og, half)
    by_acts = split3(by_stack[:tokens] * scale, axis=1)
    result += sum3(dot(by_acts[:half], own, TN) + dot(by_acts[half:], oth, TN))
    for i in range(right.shape[0]):
        right[i] = result


def gram_schmidt_kernel(gram, left_rows, out, left_columns):
    width = gram.shape[0]
    g = gram[...]
    rows = lax.broadcasted_iota(jnp.int32, (width, width), 0)
    columns = lax.broadcasted_iota(jnp.int32, (width, width), 1)
    coeffs = jnp.zeros((width, width), F32)
    products = jnp.zeros((width, width), F32)
    for k in range(width):
        along = jnp.sum(jnp.where(columns == k, products, 0.0), axis=1, keepdims=True)
        unit = (columns[:1] == k).astype(F32)
        v = unit - jnp.sum(along * coeffs, axis=0, keepdims=True)
        inner = g[k : k + 1] - jnp.sum(along * products, axis=0, keepdims=True)
        square = jnp.maximum(jnp.sum(v * inner, axis=1, keepdims=True), 0.0)
        inverse = lax.rsqrt(square + 1e-06)
        coeffs = jnp.where(rows == k, v * inverse, coeffs)
        products = jnp.where(rows == k, inner * inverse, products)
    out[...] = exact_dot(coeffs, coeffs, TN)
    for at in blocks(left_rows.shape[1]):
        left_columns[at, :] = jnp.concatenate([left_rows[:, at]] * 3, axis=0).T


def right_sum_kernel(parts, after, out, token):
    token[...] = jnp.zeros_like(token)
    total = jnp.sum(parts[...], axis=0)
    out[...] = jnp.broadcast_to(total[None], out.shape)


def final_kernel(
    inverse_replicas, place, parts, metric, left, momentum, merged, after, new_error, new_momentum,
    merged_here, slots, sems, out_sems,
):
    all_rows = blocks(merged.shape[0])
    reader = Reader([[(merged.at[at, :], merged_here.at[at, :])] for at in all_rows], sems)
    total = jnp.sum(parts[...], axis=0) * inverse_replicas
    w3 = split3(exact_dot(metric[...], total))
    writer = Writer(slots, out_sems)
    for i, at in enumerate(all_rows):
        reader.wait(i)
        writer.put((merged_here[at, :] - dot(left[at, :], w3)).astype(BF16), new_error.at[at, :])
    rows = momentum.shape[0]
    mine = pl.ds(pl.multiple_of(place[2] * rows, rows), rows)
    new_momentum[...] = (0.9 * momentum[...].astype(F32) + dot(left[mine, :], w3)).astype(BF16)
    writer.finish()


def per_device(acts, out_grad, weight, error, momentum, q_init):
    tokens, cols = out_grad.shape
    half, width = acts.shape
    rank = q_init.shape[1]
    replicas = lax.axis_size("dp")
    scale = 1.0 / tokens**0.5
    core = lax.axis_index("tensor")
    place = jnp.stack([core, 1 - core, lax.axis_index("dp")]).astype(jnp.int32)
    swap = [(0, 1), (1, 0)]
    shape = jax.ShapeDtypeStruct
    near = [[g * GROUP + i for i in range(GROUP)] for g in range(replicas // GROUP)]
    far = [[i * (replicas // GROUP) + g for i in range(GROUP)] for g in range(replicas // GROUP)]
    dma = pltpu.SemaphoreType.DMA
    n_blocks = width // BLOCK

    acts_oth = lax.ppermute(acts, "tensor", swap)

    part, pq_oth = call(
        functools.partial(left_own_kernel, scale),
        [SMEM, HBM, HBM, HBM, HBM],
        [VMEM] * 2,
        [shape((rank, width), F32), shape((3 * rank, half), BF16)],
        (place, q_init.T, out_grad, acts, error),
        flops=2 * 96 * width * 768,
        moved=13 * MIB,
        scratch=[
            pltpu.VMEM((rank, cols), F32),
            pltpu.VMEM((tokens, cols), BF16),
            pltpu.VMEM((half, width), BF16),
            pltpu.VMEM((width, cols), BF16),
            dma((n_blocks, 2)),
            dma((2,)),
        ],
    )
    left_parts, left_done = call(
        left_kernel,
        [VMEM] * 3,
        [VMEM] * 2,
        [shape((replicas, rank, CHUNK), BF16), TOKEN],
        (pq_oth, acts_oth, part),
        flops=2 * 96 * width * 256,
        moved=6 * MIB,
    )
    gathered = lax.all_to_all(left_parts, "dp", 0, 0, tiled=True)
    merged, merged_done = call(
        functools.partial(merged_kernel, scale),
        [SMEM, VMEM, HBM, HBM, HBM, VMEM],
        [HBM, VMEM],
        [pltpu.HBM((width, cols), F32), TOKEN],
        (place, out_grad, acts, acts_oth, error, left_done),
        flops=2 * tokens * cols * width,
        moved=32 * MIB,
        scratch=[
            pltpu.VMEM((half, width), BF16),
            pltpu.VMEM((half, width), BF16),
            pltpu.VMEM((width, cols), BF16),
            pltpu.VMEM((4, BLOCK, cols), F32),
            dma((n_blocks, 3)),
            dma((4,)),
        ],
    )

    left_copies, sum_done = call(
        left_sum_kernel,
        [VMEM, VMEM],
        [VMEM, VMEM],
        [shape((replicas, rank, CHUNK), BF16), TOKEN],
        (gathered, merged_done),
        flops=replicas * rank * CHUNK,
        moved=MIB,
    )
    left = lax.all_to_all(left_copies, "dp", 0, 0, tiled=True)
    own_input, oth_input, input_done = call(
        input_kernel,
        [SMEM, VMEM, HBM, VMEM],
        [HBM, HBM, VMEM],
        [pltpu.HBM((half, width), BF16), pltpu.HBM((half, width), BF16), TOKEN],
        (place, out_grad, weight, sum_done),
        flops=2 * tokens * cols * width,
        moved=17 * MIB,
        scratch=[
            pltpu.VMEM((width, cols), BF16),
            pltpu.VMEM((4, half, BLOCK), BF16),
            pltpu.VMEM((4, half, BLOCK), BF16),
            dma((n_blocks, 1)),
            dma((4,)),
            dma((4,)),
        ],
    )
    oth_input, passed = call(
        pass_kernel,
        [HBM, VMEM, VMEM],
        [HBM, VMEM],
        [pltpu.HBM((half, width), BF16), TOKEN],
        (oth_input, left, input_done),
        flops=1,
        moved=4096,
        aliases={0: 0},
    )
    received = lax.ppermute(oth_input, "tensor", swap)

    right_copies, gram, left_rows = call(
        functools.partial(right_kernel, scale),
        [SMEM, VMEM, VMEM, HBM, HBM, HBM, VMEM],
        [VMEM] * 3,
        [shape((GROUP, rank, cols), F32), shape((rank, rank), F32), shape((rank, width), BF16)],
        (place, out_grad, left, acts, acts_oth, error, passed),
        flops=2 * rank * width * 1024,
        moved=17 * MIB,
        scratch=[pltpu.VMEM((tokens + rank, width), BF16), pltpu.VMEM((width, cols), BF16), dma((n_blocks, 3))],
    )
    first = lax.all_to_all(right_copies, "dp", 0, 0, tiled=True, axis_index_groups=near)
    metric, left_columns = call(
        gram_schmidt_kernel,
        [VMEM] * 2,
        [VMEM] * 2,
        [shape((rank, rank), F32), shape((width, 3 * rank), BF16)],
        (gram, left_rows),
        flops=MIB * 1024,
        moved=3 * MIB,
    )
    second_copies, second_done = call(
        right_sum_kernel,
        [VMEM, VMEM],
        [VMEM, VMEM],
        [shape((GROUP, rank, cols), F32), TOKEN],
        (first, metric),
        flops=GROUP * rank * cols,
        moved=MIB,
    )
    second = lax.all_to_all(second_copies, "dp", 0, 0, tiled=True, axis_index_groups=far)
    input_grad, add_done = call(
        add_kernel,
        [HBM, HBM, VMEM],
        [HBM, VMEM],
        [pltpu.HBM((half, width), BF16), TOKEN],
        (own_input, received, second_done),
        flops=half * width,
        moved=12 * MIB,
        scratch=[
            pltpu.VMEM((half, width), BF16),
            pltpu.VMEM((half, width), BF16),
            pltpu.VMEM((4, half, BLOCK), BF16),
            dma((n_blocks, 2)),
            dma((4,)),
        ],
    )
    new_error, new_momentum = call(
        functools.partial(final_kernel, 1.0 / replicas),
        [SMEM, VMEM, VMEM, VMEM, VMEM, HBM, VMEM],
        [HBM, VMEM],
        [pltpu.HBM((width, cols), BF16), shape(momentum.shape, BF16)],
        (place, second, metric, left_columns, momentum, merged, add_done),
        flops=2 * 96 * width * cols,
        moved=25 * MIB,
        scratch=[pltpu.VMEM((width, cols), F32), pltpu.VMEM((4, BLOCK, cols), BF16), dma((n_blocks, 1)), dma((4,))],
    )
    return (new_error, new_momentum, input_grad)


def solution(mesh):
    return jax.shard_map(
        per_device,
        mesh=mesh,
        in_specs=(
            P(("dp", "tensor"), None),
            P("dp", "tensor"),
            P(None, "tensor"),
            P("dp", "tensor"),
            P("dp", "tensor"),
            P("tensor", None),
        ),
        out_specs=(P("dp", "tensor"), P("dp", "tensor"), P(("dp", "tensor"), None)),
        check_vma=False,
    )
```

```python
import functools

import jax
import jax.numpy as jnp
from jax import lax
from jax.experimental import pallas as pl
from jax.experimental.pallas import tpu as pltpu
from jax.sharding import PartitionSpec as P

F32 = jnp.float32
BF16 = jnp.bfloat16
MIB = 1024 * 1024
BLOCK = 1024
CHUNK = 128
GROUP = 8

NN = (((1,), (0,)), ((), ()))
NT = (((1,), (1,)), ((), ()))
TN = (((0,), (0,)), ((), ()))

VMEM = pl.BlockSpec(memory_space=pltpu.VMEM)
SMEM = pl.BlockSpec(memory_space=pltpu.SMEM)
HBM = pl.BlockSpec(memory_space=pltpu.HBM)
TOKEN = jax.ShapeDtypeStruct((8, 128), jnp.float32)


def in_hbm(x):
    return pltpu.with_memory_space_constraint(x, pltpu.HBM)


def dot(a, b, dims=NN):
    return lax.dot_general(a, b, dims, preferred_element_type=F32)


def exact_dot(a, b, dims=NN):
    return lax.dot_general(a, b, dims, precision=lax.Precision.HIGHEST, preferred_element_type=F32)


def split3(x, axis=0):
    high = x.astype(BF16)
    rest = x - high.astype(F32)
    middle = rest.astype(BF16)
    low = (rest - middle.astype(F32)).astype(BF16)
    return jnp.concatenate([high, middle, low], axis=axis)


def sum3(x):
    rows = x.shape[0] // 3
    return x[:rows] + x[rows : 2 * rows] + x[2 * rows :]


def call(kernel, in_specs, out_specs, out_shape, args, flops, moved, scratch=(), aliases={}):
    args = [in_hbm(x) if spec is HBM else x for spec, x in zip(in_specs, args)]
    return pl.pallas_call(
        kernel,
        in_specs=in_specs,
        out_specs=out_specs,
        out_shape=out_shape,
        scratch_shapes=list(scratch),
        input_output_aliases=aliases,
        compiler_params=pltpu.CompilerParams(vmem_limit_bytes=48 * MIB),
        cost_estimate=pl.CostEstimate(flops=flops, bytes_accessed=moved, transcendentals=0),
    )(*args)


def halves(place, og, half):
    own = pl.multiple_of(place[0] * half, half)
    oth = pl.multiple_of(place[1] * half, half)
    return og[pl.ds(own, half), :], og[pl.ds(oth, half), :]


def blocks(width, size=BLOCK):
    return [slice(i, i + size) for i in range(0, width, size)]


class Reader:
    def __init__(self, pairs, sems, ahead=3):
        self.ahead = ahead
        self.copies = [
            [pltpu.make_async_copy(source, target, sems.at[i, j]) for j, (source, target) in enumerate(block)]
            for i, block in enumerate(pairs)
        ]
        for block in self.copies[: self.ahead]:
            for copy in block:
                copy.start()

    def wait(self, i):
        if i + self.ahead < len(self.copies):
            for copy in self.copies[i + self.ahead]:
                copy.start()
        for copy in self.copies[i]:
            copy.wait()


class Writer:
    def __init__(self, slots, sems):
        self.slots, self.sems, self.copies = slots, sems, []

    def put(self, value, target):
        at = len(self.copies)
        slot = at % self.slots.shape[0]
        if at >= self.slots.shape[0]:
            self.copies[at - self.slots.shape[0]].wait()
        self.slots[slot] = value
        copy = pltpu.make_async_copy(self.slots.at[slot], target, self.sems.at[slot])
        copy.start()
        self.copies.append(copy)

    def finish(self):
        for copy in self.copies[-self.slots.shape[0] :]:
            copy.wait()


def left_own_kernel(
    scale, place, q_hbm, og_hbm, acts, error, part, pq_oth, q, og, acts_here, error_here, sems, small_sems
):
    half, width = acts.shape
    rows = blocks(width)
    q_copy = pltpu.make_async_copy(q_hbm, q, small_sems.at[0])
    og_copy = pltpu.make_async_copy(og_hbm, og, small_sems.at[1])
    q_copy.start()
    reads = [[(error.at[at, :], error_here.at[at, :]), (acts.at[:, at], acts_here.at[:, at])] for at in rows]
    reader = Reader(reads, sems, ahead=2)
    og_copy.start()
    q_copy.wait()
    q3 = split3(q[...])
    for i, at in enumerate(rows):
        reader.wait(i)
        by_error = sum3(dot(error_here[at, :], q3, NT).T)
        if i == 0:
            og_copy.wait()
            og_own, og_oth = halves(place, og, half)
            pq3 = split3(sum3(dot(q3, og_own, NT)) * scale)
            pq_oth[...] = split3(sum3(dot(q3, og_oth, NT)) * scale)
        part[:, at] = by_error + sum3(dot(pq3, acts_here[:, at]))


def left_kernel(pq3, acts, part, left, token):
    token[...] = jnp.zeros_like(token)
    for at in blocks(acts.shape[1]):
        total = part[:, at] + sum3(dot(pq3[...], acts[:, at]))
        for i in range(BLOCK // CHUNK):
            left[at.start // CHUNK + i] = total[:, i * CHUNK : (i + 1) * CHUNK].astype(BF16)


def input_oth_kernel(place, og, weight, after, part, token, weight_here, slots, sems, out_sems):
    token[...] = jnp.zeros_like(token)
    half, width = part.shape
    rows = blocks(width)
    reader = Reader([[(weight.at[at, :], weight_here.at[at, :])] for at in rows], sems)
    _, oth = halves(place, og, half)
    writer = Writer(slots, out_sems)
    for i, at in enumerate(rows):
        reader.wait(i)
        writer.put(dot(oth, weight_here[at, :], NT).astype(BF16), part.at[:, at])
    writer.finish()


def pass_kernel(part, after, out):
    pass


def input_own_kernel(
    place, og, weight, received, gram, out, metric, token, weight_here, received_here, slots, sems, out_sems
):
    token[...] = jnp.zeros_like(token)
    half, width = received.shape
    rank = gram.shape[0]
    rows = blocks(width)
    reader = Reader(
        [[(weight.at[at, :], weight_here.at[at, :]), (received.at[:, at], received_here.at[:, at])] for at in rows],
        sems,
    )
    own, _ = halves(place, og, half)
    writer = Writer(slots, out_sems)
    steps = gram_schmidt(gram[...])
    for i, at in enumerate(rows):
        reader.wait(i)
        product = dot(own, weight_here[at, :], NT).astype(BF16)
        for _ in range(rank * i // len(rows), rank * (i + 1) // len(rows)):
            coeffs = next(steps)
        writer.put((product.astype(F32) + received_here[:, at].astype(F32)).astype(BF16), out.at[:, at])
    metric[...] = exact_dot(coeffs, coeffs, NT)
    writer.finish()


def left_sum_kernel(parts, after, out, token):
    token[...] = jnp.zeros_like(token)
    total = jnp.sum(parts[...].astype(F32), axis=0).astype(BF16)
    out[...] = jnp.broadcast_to(total[None], out.shape)


def right_kernel(
    scale, place, og, left, acts, acts_oth, error, right, gram, left_rows, stack, error_here, sems
):
    tokens, cols = og.shape
    half, width = acts.shape
    rows = blocks(width, BLOCK // 2)
    reader = Reader(
        [
            [
                (acts.at[:, at], stack.at[:half, at]),
                (acts_oth.at[:, at], stack.at[half:tokens, at]),
                (error.at[at, :], error_here.at[at, :]),
            ]
            for at in rows
        ],
        sems,
        ahead=8,
    )
    for i in range(left.shape[0]):
        stack[tokens:, i * CHUNK : (i + 1) * CHUNK] = left[i]
    left_rows[...] = stack[tokens:, :]
    by_stack, result = None, None
    for i, at in enumerate(rows):
        reader.wait(i)
        here = stack[tokens:, at]
        stack_term = dot(stack[:, at], here, NT)
        error_term = dot(here, error_here[at, :])
        by_stack = stack_term if by_stack is None else by_stack + stack_term
        result = error_term if result is None else result + error_term
    gram[...] = by_stack[tokens:]
    own, oth = halves(place, og, half)
    by_acts = split3(by_stack[:tokens] * scale, axis=1)
    result += sum3(dot(by_acts[:half], own, TN) + dot(by_acts[half:], oth, TN))
    for i in range(right.shape[0]):
        right[i] = result


def gram_schmidt(g):
    width = g.shape[0]
    rows = lax.broadcasted_iota(jnp.int32, (width, width), 0)
    columns = lax.broadcasted_iota(jnp.int32, (width, width), 1)
    coeffs = jnp.zeros((width, width), F32)
    products = jnp.zeros((width, width), F32)
    for k in range(width):
        along = products[k : k + 1]
        unit = (rows[:, :1] == k).astype(F32)
        v = unit - jnp.sum(along * coeffs, axis=1, keepdims=True)
        inner = g[:, k : k + 1] - jnp.sum(along * products, axis=1, keepdims=True)
        square = jnp.maximum(jnp.sum(v * inner, axis=0, keepdims=True), 0.0)
        inverse = lax.rsqrt(square + 1e-06)
        coeffs = jnp.where(columns == k, v * inverse, coeffs)
        products = jnp.where(columns == k, inner * inverse, products)
        yield coeffs


def right_sum_kernel(parts, after, out):
    total = jnp.sum(parts[...], axis=0)
    out[...] = jnp.broadcast_to(total[None], out.shape)


def final_kernel(
    scale, inverse_replicas, place, parts, metric, og, left_rows, momentum, acts, acts_oth, error,
    new_error, new_momentum, stack, rest, error_here, slots, sems, out_sems,
):
    tokens, cols = og.shape
    half, width = acts.shape
    rank = left_rows.shape[0]
    rows = blocks(width)
    reader = Reader(
        [
            [
                (acts.at[:, at], stack.at[:half, at]),
                (acts_oth.at[:, at], stack.at[half:tokens, at]),
                (error.at[at, :], error_here.at[at, :]),
            ]
            for at in rows
        ],
        sems,
    )
    for i in range(3):
        stack[tokens + i * rank : tokens + (i + 1) * rank, :] = left_rows[...]
    total = jnp.sum(parts[...], axis=0) * (-inverse_replicas / scale)
    own, oth = halves(place, og, half)
    rest[:half] = own
    rest[half:tokens] = oth
    rest[tokens:] = split3(exact_dot(metric[...], total))
    writer = Writer(slots, out_sems)
    for i, at in enumerate(rows):
        reader.wait(i)
        product = dot(stack[:, at], rest[...], TN)
        writer.put((product * scale + error_here[at, :].astype(F32)).astype(BF16), new_error.at[at, :])
    count = momentum.shape[0]
    mine = pl.ds(pl.multiple_of(place[2] * count, count), count)
    approx = dot(stack[tokens:, mine], rest[tokens:], TN) * -scale
    new_momentum[...] = (0.9 * momentum[...].astype(F32) + approx).astype(BF16)
    writer.finish()


def per_device(acts, out_grad, weight, error, momentum, q_init):
    tokens, cols = out_grad.shape
    half, width = acts.shape
    rank = q_init.shape[1]
    replicas = lax.axis_size("dp")
    scale = 1.0 / tokens**0.5
    core = lax.axis_index("tensor")
    place = jnp.stack([core, 1 - core, lax.axis_index("dp")]).astype(jnp.int32)
    swap = [(0, 1), (1, 0)]
    shape = jax.ShapeDtypeStruct
    near = [[g * GROUP + i for i in range(GROUP)] for g in range(replicas // GROUP)]
    far = [[i * (replicas // GROUP) + g for i in range(GROUP)] for g in range(replicas // GROUP)]
    dma = pltpu.SemaphoreType.DMA
    n_blocks = width // BLOCK

    acts_oth = lax.ppermute(acts, "tensor", swap)

    part, pq_oth = call(
        functools.partial(left_own_kernel, scale),
        [SMEM, HBM, HBM, HBM, HBM],
        [VMEM] * 2,
        [shape((rank, width), F32), shape((3 * rank, half), BF16)],
        (place, q_init.T, out_grad, acts, error),
        flops=2 * 96 * width * 768,
        moved=13 * MIB,
        scratch=[
            pltpu.VMEM((rank, cols), F32),
            pltpu.VMEM((tokens, cols), BF16),
            pltpu.VMEM((half, width), BF16),
            pltpu.VMEM((width, cols), BF16),
            dma((n_blocks, 2)),
            dma((2,)),
        ],
    )
    left_parts, left_done = call(
        left_kernel,
        [VMEM] * 3,
        [VMEM] * 2,
        [shape((replicas, rank, CHUNK), BF16), TOKEN],
        (pq_oth, acts_oth, part),
        flops=2 * 96 * width * 256,
        moved=6 * MIB,
    )
    gathered = lax.all_to_all(left_parts, "dp", 0, 0, tiled=True)
    oth_input, oth_done = call(
        input_oth_kernel,
        [SMEM, VMEM, HBM, VMEM],
        [HBM, VMEM],
        [pltpu.HBM((half, width), BF16), TOKEN],
        (place, out_grad, weight, left_done),
        flops=tokens * cols * width,
        moved=13 * MIB,
        scratch=[
            pltpu.VMEM((width, cols), BF16),
            pltpu.VMEM((4, half, BLOCK), BF16),
            dma((n_blocks, 1)),
            dma((4,)),
        ],
    )

    left_copies, sum_done = call(
        left_sum_kernel,
        [VMEM, VMEM],
        [VMEM, VMEM],
        [shape((replicas, rank, CHUNK), BF16), TOKEN],
        (gathered, oth_done),
        flops=replicas * rank * CHUNK,
        moved=MIB,
    )
    left = lax.all_to_all(left_copies, "dp", 0, 0, tiled=True)
    oth_input = call(
        pass_kernel,
        [HBM, VMEM],
        HBM,
        pltpu.HBM((half, width), BF16),
        (oth_input, sum_done),
        flops=1,
        moved=4096,
        aliases={0: 0},
    )
    received = lax.ppermute(oth_input, "tensor", swap)

    right_copies, gram, left_rows = call(
        functools.partial(right_kernel, scale),
        [SMEM, VMEM, VMEM, HBM, HBM, HBM],
        [VMEM] * 3,
        [shape((GROUP, rank, cols), F32), shape((rank, rank), F32), shape((rank, width), BF16)],
        (place, out_grad, left, acts, acts_oth, error),
        flops=2 * rank * width * 1024,
        moved=17 * MIB,
        scratch=[pltpu.VMEM((tokens + rank, width), BF16), pltpu.VMEM((width, cols), BF16), dma((2 * n_blocks, 3))],
    )
    first = lax.all_to_all(right_copies, "dp", 0, 0, tiled=True, axis_index_groups=near)
    input_grad, metric, input_done = call(
        input_own_kernel,
        [SMEM, VMEM, HBM, HBM, VMEM],
        [HBM, VMEM, VMEM],
        [pltpu.HBM((half, width), BF16), shape((rank, rank), F32), TOKEN],
        (place, out_grad, weight, received, gram),
        flops=tokens * cols * width,
        moved=17 * MIB,
        scratch=[
            pltpu.VMEM((width, cols), BF16),
            pltpu.VMEM((half, width), BF16),
            pltpu.VMEM((4, half, BLOCK), BF16),
            dma((n_blocks, 2)),
            dma((4,)),
        ],
    )
    second_copies = call(
        right_sum_kernel,
        [VMEM, VMEM],
        VMEM,
        shape((GROUP, rank, cols), F32),
        (first, input_done),
        flops=GROUP * rank * cols,
        moved=MIB,
    )
    second = lax.all_to_all(second_copies, "dp", 0, 0, tiled=True, axis_index_groups=far)
    new_error, new_momentum = call(
        functools.partial(final_kernel, scale, 1.0 / replicas),
        [SMEM, VMEM, VMEM, VMEM, VMEM, VMEM, HBM, HBM, HBM],
        [HBM, VMEM],
        [pltpu.HBM((width, cols), BF16), shape(momentum.shape, BF16)],
        (place, second, metric, out_grad, left_rows, momentum, acts, acts_oth, error),
        flops=2 * (tokens + 3 * rank) * width * cols,
        moved=25 * MIB,
        scratch=[
            pltpu.VMEM((tokens + 3 * rank, width), BF16),
            pltpu.VMEM((tokens + 3 * rank, cols), BF16),
            pltpu.VMEM((width, cols), BF16),
            pltpu.VMEM((4, BLOCK, cols), BF16),
            dma((n_blocks, 3)),
            dma((4,)),
        ],
    )
    return (new_error, new_momentum, input_grad)


def solution(mesh):
    return jax.shard_map(
        per_device,
        mesh=mesh,
        in_specs=(
            P(("dp", "tensor"), None),
            P("dp", "tensor"),
            P(None, "tensor"),
            P("dp", "tensor"),
            P("dp", "tensor"),
            P("tensor", None),
        ),
        out_specs=(P("dp", "tensor"), P("dp", "tensor"), P(("dp", "tensor"), None)),
        check_vma=False,
    )
```

```python
import functools

import jax
import jax.numpy as jnp
from jax import lax
from jax.experimental import pallas as pl
from jax.experimental.pallas import tpu as pltpu
from jax.sharding import PartitionSpec as P

F32 = jnp.float32
BF16 = jnp.bfloat16
MIB = 1024 * 1024
BLOCK = 1024
CHUNK = 128
GROUP = 8

NN = (((1,), (0,)), ((), ()))
NT = (((1,), (1,)), ((), ()))
TN = (((0,), (0,)), ((), ()))

VMEM = pl.BlockSpec(memory_space=pltpu.VMEM)
HBM = pl.BlockSpec(memory_space=pltpu.HBM)
TOKEN = jax.ShapeDtypeStruct((8, 128), jnp.float32)


def in_hbm(x):
    return pltpu.with_memory_space_constraint(x, pltpu.HBM)


def dot(a, b, dims=NN):
    return lax.dot_general(a, b, dims, preferred_element_type=F32)


def exact_dot(a, b, dims=NN):
    return lax.dot_general(a, b, dims, precision=lax.Precision.HIGHEST, preferred_element_type=F32)


def split3(x, axis=0):
    high = x.astype(BF16)
    rest = x - high.astype(F32)
    middle = rest.astype(BF16)
    low = (rest - middle.astype(F32)).astype(BF16)
    return jnp.concatenate([high, middle, low], axis=axis)


def sum3(x):
    rows = x.shape[0] // 3
    return x[:rows] + x[rows : 2 * rows] + x[2 * rows :]


def call(kernel, in_specs, out_specs, out_shape, args, flops, moved, scratch=(), aliases={}):
    args = [in_hbm(x) if spec is HBM else x for spec, x in zip(in_specs, args)]
    return pl.pallas_call(
        kernel,
        in_specs=in_specs,
        out_specs=out_specs,
        out_shape=out_shape,
        scratch_shapes=list(scratch),
        input_output_aliases=aliases,
        compiler_params=pltpu.CompilerParams(vmem_limit_bytes=48 * MIB),
        cost_estimate=pl.CostEstimate(flops=flops, bytes_accessed=moved, transcendentals=0),
    )(*args)


def halves(og, half):
    core = lax.axis_index("tensor")
    own = pl.multiple_of(core * half, half)
    oth = pl.multiple_of((1 - core) * half, half)
    return og[pl.ds(own, half), :], og[pl.ds(oth, half), :]


def blocks(width, size=BLOCK):
    return [slice(i, i + size) for i in range(0, width, size)]


class Reader:
    def __init__(self, pairs, sems, ahead=3):
        self.ahead = ahead
        self.copies = [
            [pltpu.make_async_copy(source, target, sems.at[i, j]) for j, (source, target) in enumerate(block)]
            for i, block in enumerate(pairs)
        ]
        for block in self.copies[: self.ahead]:
            for copy in block:
                copy.start()

    def wait(self, i):
        if i + self.ahead < len(self.copies):
            for copy in self.copies[i + self.ahead]:
                copy.start()
        for copy in self.copies[i]:
            copy.wait()


class Writer:
    def __init__(self, slots, sems):
        self.slots, self.sems, self.copies = slots, sems, []

    def put(self, value, target):
        at = len(self.copies)
        slot = at % self.slots.shape[0]
        if at >= self.slots.shape[0]:
            self.copies[at - self.slots.shape[0]].wait()
        rows = value.shape[0]
        self.slots[slot, :rows] = value
        copy = pltpu.make_async_copy(self.slots.at[slot, :rows], target, self.sems.at[slot])
        copy.start()
        self.copies.append(copy)

    def finish(self):
        for copy in self.copies[-self.slots.shape[0] :]:
            copy.wait()


def left_own_kernel(
    scale, q_hbm, og_hbm, acts, error, part, pq_oth, q, og, acts_here, error_here, sems, small_sems
):
    half, width = acts.shape
    rows = blocks(width)
    q_copy = pltpu.make_async_copy(q_hbm, q, small_sems.at[0])
    og_copy = pltpu.make_async_copy(og_hbm, og, small_sems.at[1])
    q_copy.start()
    reads = [[(error.at[at, :], error_here.at[at, :]), (acts.at[:, at], acts_here.at[:, at])] for at in rows]
    reader = Reader(reads, sems, ahead=2)
    og_copy.start()
    q_copy.wait()
    q3 = split3(q[...])
    for i, at in enumerate(rows):
        reader.wait(i)
        by_error = sum3(dot(error_here[at, :], q3, NT).T)
        if i == 0:
            og_copy.wait()
            og_own, og_oth = halves(og, half)
            pq3 = split3(sum3(dot(q3, og_own, NT)) * scale)
            pq_oth[...] = split3(sum3(dot(q3, og_oth, NT)) * scale)
        part[:, at] = by_error + sum3(dot(pq3, acts_here[:, at]))


def left_kernel(pq3, acts, part, left, acts_kept, token, here, sems):
    token[...] = jnp.zeros_like(token)
    rows = blocks(acts.shape[1])
    copies = [pltpu.make_async_copy(acts, acts_kept, sems.at[len(rows)])]
    copies[0].start()
    for i, at in enumerate(rows):
        total = part[:, at] + sum3(dot(pq3[...], acts[:, at]))
        count = BLOCK // CHUNK
        chunks = slice(i * count, (i + 1) * count)
        for j in range(count):
            here[i * count + j] = total[:, j * CHUNK : (j + 1) * CHUNK].astype(BF16)
        copies.append(pltpu.make_async_copy(here.at[chunks], left.at[chunks], sems.at[i]))
        copies[-1].start()
    for copy in copies:
        copy.wait()


def input_oth_kernel(og, weight, after, part, token, weight_here, slots, sems, out_sems):
    token[...] = jnp.zeros_like(token)
    half, width = part.shape
    rows = blocks(width)
    reader = Reader([[(weight.at[at, :], weight_here.at[at, :])] for at in rows], sems)
    _, oth = halves(og, half)
    writer = Writer(slots, out_sems)
    for i, at in enumerate(rows):
        reader.wait(i)
        writer.put(dot(oth, weight_here[at, :], NT).astype(BF16), part.at[:, at])
    writer.finish()


def pass_kernel(part, after, out):
    pass


def input_own_kernel(
    og, weight, received, gram, out, metric, token, weight_here, received_here, slots, sems, out_sems
):
    token[...] = jnp.zeros_like(token)
    half, width = received.shape
    rank = gram.shape[0]
    rows = blocks(width)
    reader = Reader(
        [[(weight.at[at, :], weight_here.at[at, :]), (received.at[:, at], received_here.at[:, at])] for at in rows],
        sems,
    )
    own, _ = halves(og, half)
    writer = Writer(slots, out_sems)
    steps = gram_schmidt(gram[...])
    first = rank // 4
    for _ in range(first):
        coeffs = next(steps)
    for i, at in enumerate(rows):
        reader.wait(i)
        product = dot(own, weight_here[at, :], NT).astype(BF16)
        for _ in range((rank - first) * i // len(rows), (rank - first) * (i + 1) // len(rows)):
            coeffs = next(steps)
        writer.put((product.astype(F32) + received_here[:, at].astype(F32)).astype(BF16), out.at[:, at])
    metric[...] = exact_dot(coeffs, coeffs, NT)
    writer.finish()


def left_sum_kernel(parts, after, out, token):
    token[...] = jnp.zeros_like(token)
    total = jnp.sum(parts[...].astype(F32), axis=0).astype(BF16)
    out[...] = jnp.broadcast_to(total[None], out.shape)


def right_kernel(
    scale, og, left, acts, acts_oth, error, right, gram, left_rows, stack, error_here, right_here, sems, out_sems
):
    tokens, cols = og.shape
    half, width = acts.shape
    rows = blocks(width, BLOCK // 2)
    reader = Reader(
        [
            [
                (acts.at[:, at], stack.at[:half, at]),
                (acts_oth.at[:, at], stack.at[half:tokens, at]),
                (error.at[at, :], error_here.at[at, :]),
            ]
            for at in rows
        ],
        sems,
        ahead=8,
    )
    for i in range(left.shape[0]):
        stack[tokens:, i * CHUNK : (i + 1) * CHUNK] = left[i]
    left_copy = pltpu.make_async_copy(stack.at[tokens:, :], left_rows, out_sems.at[0])
    left_copy.start()
    by_stack, result = None, None
    for i, at in enumerate(rows):
        reader.wait(i)
        here = stack[tokens:, at]
        stack_term = dot(stack[:, at], here, NT)
        error_term = dot(here, error_here[at, :])
        by_stack = stack_term if by_stack is None else by_stack + stack_term
        result = error_term if result is None else result + error_term
    gram[...] = by_stack[tokens:]
    own, oth = halves(og, half)
    by_acts = split3(by_stack[:tokens] * scale, axis=1)
    result += sum3(dot(by_acts[:half], own, TN) + dot(by_acts[half:], oth, TN))
    right_here[...] = result
    copies = [
        pltpu.make_async_copy(right_here, right.at[i], out_sems.at[1 + i]) for i in range(right.shape[0])
    ]
    for copy in copies:
        copy.start()
    for copy in copies:
        copy.wait()
    left_copy.wait()


def gram_schmidt(g):
    width = g.shape[0]
    rows = lax.broadcasted_iota(jnp.int32, (width, width), 0)
    columns = lax.broadcasted_iota(jnp.int32, (width, width), 1)
    coeffs = jnp.zeros((width, width), F32)
    products = jnp.zeros((width, width), F32)
    for k in range(width):
        along = products[k : k + 1]
        unit = (rows[:, :1] == k).astype(F32)
        v = unit - jnp.sum(along * coeffs, axis=1, keepdims=True)
        inner = g[:, k : k + 1] - jnp.sum(along * products, axis=1, keepdims=True)
        square = jnp.maximum(jnp.sum(v * inner, axis=0, keepdims=True), 0.0)
        inverse = lax.rsqrt(square + 1e-06)
        coeffs = jnp.where(columns == k, v * inverse, coeffs)
        products = jnp.where(columns == k, inner * inverse, products)
        yield coeffs


def right_sum_kernel(parts, after, out):
    total = jnp.sum(parts[...], axis=0)
    out[...] = jnp.broadcast_to(total[None], out.shape)


def final_kernel(
    scale, inverse_replicas, parts, metric, og, left_rows, momentum, acts, acts_oth, error,
    new_error, new_momentum, stack, rest, error_here, slots, sems, out_sems,
):
    tokens, cols = og.shape
    half, width = acts.shape
    rank = left_rows.shape[0]
    rows = blocks(width)
    reader = Reader(
        [
            [
                (acts.at[:, at], stack.at[:half, at]),
                (acts_oth.at[:, at], stack.at[half:tokens, at]),
                (error.at[at, :], error_here.at[at, :]),
            ]
            for at in rows
        ],
        sems,
    )
    for i in range(3):
        stack[tokens + i * rank : tokens + (i + 1) * rank, :] = left_rows[...]
    total = jnp.sum(parts[...], axis=0) * (-inverse_replicas / scale)
    own, oth = halves(og, half)
    rest[:half] = own
    rest[half:tokens] = oth
    rest[tokens:] = split3(exact_dot(metric[...], total))
    writer = Writer(slots, out_sems)
    for i, at in enumerate(rows):
        reader.wait(i)
        product = dot(stack[:, at], rest[...], TN)
        writer.put((product * scale + error_here[at, :].astype(F32)).astype(BF16), new_error.at[at, :])
    count = momentum.shape[0]
    mine = pl.ds(pl.multiple_of(lax.axis_index("dp") * count, count), count)
    approx = dot(stack[tokens:, mine], rest[tokens:], TN) * -scale
    new_momentum[...] = (0.9 * momentum[...].astype(F32) + approx).astype(BF16)
    writer.finish()


def per_device(acts, out_grad, weight, error, momentum, q_init):
    tokens, cols = out_grad.shape
    half, width = acts.shape
    rank = q_init.shape[1]
    replicas = lax.axis_size("dp")
    scale = 1.0 / tokens**0.5
    swap = [(0, 1), (1, 0)]
    shape = jax.ShapeDtypeStruct
    near = [[g * GROUP + i for i in range(GROUP)] for g in range(replicas // GROUP)]
    far = [[i * (replicas // GROUP) + g for i in range(GROUP)] for g in range(replicas // GROUP)]
    dma = pltpu.SemaphoreType.DMA
    n_blocks = width // BLOCK

    acts_oth = lax.ppermute(acts, "tensor", swap)

    part, pq_oth = call(
        functools.partial(left_own_kernel, scale),
        [HBM, HBM, HBM, HBM],
        [VMEM] * 2,
        [shape((rank, width), F32), shape((3 * rank, half), BF16)],
        (q_init.T, out_grad, acts, error),
        flops=2 * 96 * width * 768,
        moved=13 * MIB,
        scratch=[
            pltpu.VMEM((rank, cols), F32),
            pltpu.VMEM((tokens, cols), BF16),
            pltpu.VMEM((half, width), BF16),
            pltpu.VMEM((width, cols), BF16),
            dma((n_blocks, 2)),
            dma((2,)),
        ],
    )
    left_parts, acts_oth, left_done = call(
        left_kernel,
        [VMEM] * 3,
        [HBM, HBM, VMEM],
        [pltpu.HBM((replicas, rank, CHUNK), BF16), pltpu.HBM((half, width), BF16), TOKEN],
        (pq_oth, acts_oth, part),
        flops=2 * 96 * width * 256,
        moved=6 * MIB,
        scratch=[pltpu.VMEM((replicas, rank, CHUNK), BF16), dma((n_blocks + 1,))],
    )
    gathered = lax.all_to_all(left_parts, "dp", 0, 0, tiled=True)
    oth_input, oth_done = call(
        input_oth_kernel,
        [VMEM, HBM, VMEM],
        [HBM, VMEM],
        [pltpu.HBM((half, width), BF16), TOKEN],
        (out_grad, weight, left_done),
        flops=tokens * cols * width,
        moved=13 * MIB,
        scratch=[
            pltpu.VMEM((width, cols), BF16),
            pltpu.VMEM((4, half, BLOCK), BF16),
            dma((n_blocks, 1)),
            dma((4,)),
        ],
    )

    left_copies, sum_done = call(
        left_sum_kernel,
        [VMEM, VMEM],
        [VMEM, VMEM],
        [shape((replicas, rank, CHUNK), BF16), TOKEN],
        (gathered, oth_done),
        flops=replicas * rank * CHUNK,
        moved=MIB,
    )
    left = lax.all_to_all(left_copies, "dp", 0, 0, tiled=True)
    oth_input = call(
        pass_kernel,
        [HBM, VMEM],
        HBM,
        pltpu.HBM((half, width), BF16),
        (oth_input, sum_done),
        flops=1,
        moved=4096,
        aliases={0: 0},
    )
    received = lax.ppermute(oth_input, "tensor", swap)

    right_copies, gram, left_rows = call(
        functools.partial(right_kernel, scale),
        [VMEM, VMEM, HBM, HBM, HBM],
        [HBM, VMEM, HBM],
        [pltpu.HBM((GROUP, rank, cols), F32), shape((rank, rank), F32), pltpu.HBM((rank, width), BF16)],
        (out_grad, left, acts, acts_oth, error),
        flops=2 * rank * width * 1024,
        moved=17 * MIB,
        scratch=[pltpu.VMEM((tokens + rank, width), BF16), pltpu.VMEM((width, cols), BF16), pltpu.VMEM((rank, cols), F32), dma((2 * n_blocks, 3)), dma((1 + GROUP,))],
    )
    first = lax.all_to_all(right_copies, "dp", 0, 0, tiled=True, axis_index_groups=near)
    input_grad, metric, input_done = call(
        input_own_kernel,
        [VMEM, HBM, HBM, VMEM],
        [HBM, VMEM, VMEM],
        [pltpu.HBM((half, width), BF16), shape((rank, rank), F32), TOKEN],
        (out_grad, weight, received, gram),
        flops=tokens * cols * width,
        moved=17 * MIB,
        scratch=[
            pltpu.VMEM((width, cols), BF16),
            pltpu.VMEM((half, width), BF16),
            pltpu.VMEM((4, half, BLOCK), BF16),
            dma((n_blocks, 2)),
            dma((4,)),
        ],
    )
    second_copies = call(
        right_sum_kernel,
        [VMEM, VMEM],
        VMEM,
        shape((GROUP, rank, cols), F32),
        (first, input_done),
        flops=GROUP * rank * cols,
        moved=MIB,
    )
    second = lax.all_to_all(second_copies, "dp", 0, 0, tiled=True, axis_index_groups=far)
    new_error, new_momentum = call(
        functools.partial(final_kernel, scale, 1.0 / replicas),
        [VMEM, VMEM, VMEM, VMEM, VMEM, HBM, HBM, HBM],
        [HBM, VMEM],
        [pltpu.HBM((width, cols), BF16), shape(momentum.shape, BF16)],
        (second, metric, out_grad, left_rows, momentum, acts, acts_oth, error),
        flops=2 * (tokens + 3 * rank) * width * cols,
        moved=25 * MIB,
        scratch=[
            pltpu.VMEM((tokens + 3 * rank, width), BF16),
            pltpu.VMEM((tokens + 3 * rank, cols), BF16),
            pltpu.VMEM((width, cols), BF16),
            pltpu.VMEM((4, BLOCK, cols), BF16),
            dma((n_blocks, 3)),
            dma((4,)),
        ],
    )
    return (new_error, new_momentum, input_grad)


def solution(mesh):
    return jax.shard_map(
        per_device,
        mesh=mesh,
        in_specs=(
            P(("dp", "tensor"), None),
            P("dp", "tensor"),
            P(None, "tensor"),
            P("dp", "tensor"),
            P("dp", "tensor"),
            P("tensor", None),
        ),
        out_specs=(P("dp", "tensor"), P("dp", "tensor"), P(("dp", "tensor"), None)),
        check_vma=False,
    )
```

```python
import functools

import jax
import jax.numpy as jnp
from jax import lax
from jax.experimental import pallas as pl
from jax.experimental.pallas import tpu as pltpu
from jax.sharding import PartitionSpec as P

F32 = jnp.float32
BF16 = jnp.bfloat16
MIB = 1024 * 1024
BLOCK = 1024
CHUNK = 128

NN = (((1,), (0,)), ((), ()))
NT = (((1,), (1,)), ((), ()))
TN = (((0,), (0,)), ((), ()))

VMEM = pl.BlockSpec(memory_space=pltpu.VMEM)
HBM = pl.BlockSpec(memory_space=pltpu.HBM)
TOKEN = jax.ShapeDtypeStruct((8, 128), jnp.float32)


def in_hbm(x):
    return pltpu.with_memory_space_constraint(x, pltpu.HBM)


def dot(a, b, dims=NN):
    return lax.dot_general(a, b, dims, preferred_element_type=F32)


def exact_dot(a, b, dims=NN):
    return lax.dot_general(a, b, dims, precision=lax.Precision.HIGHEST, preferred_element_type=F32)


def split3(x, axis=0):
    high = x.astype(BF16)
    rest = x - high.astype(F32)
    middle = rest.astype(BF16)
    low = (rest - middle.astype(F32)).astype(BF16)
    return jnp.concatenate([high, middle, low], axis=axis)


def sum3(x):
    rows = x.shape[0] // 3
    return x[:rows] + x[rows : 2 * rows] + x[2 * rows :]


def call(kernel, in_specs, out_specs, out_shape, args, flops, moved, scratch=(), aliases={}):
    args = [in_hbm(x) if spec is HBM else x for spec, x in zip(in_specs, args)]
    return pl.pallas_call(
        kernel,
        in_specs=in_specs,
        out_specs=out_specs,
        out_shape=out_shape,
        scratch_shapes=list(scratch),
        input_output_aliases=aliases,
        compiler_params=pltpu.CompilerParams(vmem_limit_bytes=48 * MIB),
        cost_estimate=pl.CostEstimate(flops=flops, bytes_accessed=moved, transcendentals=0),
    )(*args)


def halves(og, half):
    core = lax.axis_index("tensor")
    own = pl.multiple_of(core * half, half)
    oth = pl.multiple_of((1 - core) * half, half)
    return og[pl.ds(own, half), :], og[pl.ds(oth, half), :]


def blocks(width, size=BLOCK):
    return [slice(i, i + size) for i in range(0, width, size)]


class Reader:
    def __init__(self, pairs, sems, ahead=3):
        self.ahead = ahead
        self.copies = [
            [pltpu.make_async_copy(source, target, sems.at[i, j]) for j, (source, target) in enumerate(block)]
            for i, block in enumerate(pairs)
        ]
        for block in self.copies[: self.ahead]:
            for copy in block:
                copy.start()

    def wait(self, i):
        if i + self.ahead < len(self.copies):
            for copy in self.copies[i + self.ahead]:
                copy.start()
        for copy in self.copies[i]:
            copy.wait()


class Writer:
    def __init__(self, slots, sems):
        self.slots, self.sems, self.copies = slots, sems, []

    def put(self, value, target):
        at = len(self.copies)
        slot = at % self.slots.shape[0]
        if at >= self.slots.shape[0]:
            self.copies[at - self.slots.shape[0]].wait()
        rows = value.shape[0]
        self.slots[slot, :rows] = value
        copy = pltpu.make_async_copy(self.slots.at[slot, :rows], target, self.sems.at[slot])
        copy.start()
        self.copies.append(copy)

    def finish(self):
        for copy in self.copies[-self.slots.shape[0] :]:
            copy.wait()


def left_own_kernel(
    scale, q_hbm, og_hbm, acts, error, part, pq_oth, q, og, acts_here, error_here, sems, small_sems
):
    half, width = acts.shape
    rows = blocks(width)
    q_copy = pltpu.make_async_copy(q_hbm, q, small_sems.at[0])
    og_copy = pltpu.make_async_copy(og_hbm, og, small_sems.at[1])
    q_copy.start()
    reads = [[(error.at[at, :], error_here.at[at, :]), (acts.at[:, at], acts_here.at[:, at])] for at in rows]
    reader = Reader(reads, sems, ahead=2)
    og_copy.start()
    q_copy.wait()
    q3 = split3(q[...])
    for i, at in enumerate(rows):
        reader.wait(i)
        by_error = sum3(dot(error_here[at, :], q3, NT).T)
        if i == 0:
            og_copy.wait()
            og_own, og_oth = halves(og, half)
            pq3 = split3(sum3(dot(q3, og_own, NT)) * scale)
            pq_oth[...] = split3(sum3(dot(q3, og_oth, NT)) * scale)
        part[:, at] = by_error + sum3(dot(pq3, acts_here[:, at]))


def left_kernel(pq3, acts, part, left, acts_kept, token, here, sems):
    token[...] = jnp.zeros_like(token)
    rows = blocks(acts.shape[1])
    copies = [pltpu.make_async_copy(acts, acts_kept, sems.at[len(rows)])]
    copies[0].start()
    for i, at in enumerate(rows):
        total = part[:, at] + sum3(dot(pq3[...], acts[:, at]))
        count = BLOCK // CHUNK
        chunks = slice(i * count, (i + 1) * count)
        for j in range(count):
            here[i * count + j] = total[:, j * CHUNK : (j + 1) * CHUNK].astype(BF16)
        copies.append(pltpu.make_async_copy(here.at[chunks], left.at[chunks], sems.at[i]))
        copies[-1].start()
    for copy in copies:
        copy.wait()


def input_oth_kernel(og, weight, after, part, token, weight_here, slots, sems, out_sems):
    token[...] = jnp.zeros_like(token)
    half, width = part.shape
    rows = blocks(width)
    reader = Reader([[(weight.at[at, :], weight_here.at[at, :])] for at in rows], sems)
    _, oth = halves(og, half)
    writer = Writer(slots, out_sems)
    for i, at in enumerate(rows):
        reader.wait(i)
        writer.put(dot(oth, weight_here[at, :], NT).astype(BF16), part.at[:, at])
    writer.finish()


def pass_kernel(part, after, out):
    pass


def input_own_kernel(part, og, weight, received, after, *refs):
    out, token, weight_here, slots, sems, out_sems = refs[part:]
    token[...] = jnp.zeros_like(token)
    half, width = received.shape
    rows = blocks(width)
    rows = rows[: len(rows) // 2] if part == 0 else rows[len(rows) // 2 :]
    reader = Reader([[(weight.at[at, :], weight_here.at[at, :])] for at in rows], sems)
    own, _ = halves(og, half)
    writer = Writer(slots, out_sems)
    for i, at in enumerate(rows):
        reader.wait(i)
        product = dot(own, weight_here[at, :], NT).astype(BF16)
        writer.put((product.astype(F32) + received[:, at].astype(F32)).astype(BF16), out.at[:, at])
    writer.finish()


def gram_schmidt_kernel(gram, metric):
    for coeffs in gram_schmidt(gram[...]):
        pass
    metric[...] = exact_dot(coeffs, coeffs, NT)


def left_sum_kernel(parts, after, out):
    total = jnp.sum(parts[...].astype(F32), axis=0).astype(BF16)
    out[...] = jnp.broadcast_to(total[None], out.shape)


def right_kernel(
    scale, og, left, acts, acts_oth, error, right, gram, left_rows, stack, error_here, sems, out_sems
):
    tokens, cols = og.shape
    half, width = acts.shape
    rows = blocks(width, BLOCK // 2)
    reader = Reader(
        [
            [
                (acts.at[:, at], stack.at[:half, at]),
                (acts_oth.at[:, at], stack.at[half:tokens, at]),
                (error.at[at, :], error_here.at[at, :]),
            ]
            for at in rows
        ],
        sems,
        ahead=8,
    )
    for i in range(left.shape[0]):
        stack[tokens:, i * CHUNK : (i + 1) * CHUNK] = left[i]
    left_copy = pltpu.make_async_copy(stack.at[tokens:, :], left_rows, out_sems.at[0])
    left_copy.start()
    by_stack, result = None, None
    for i, at in enumerate(rows):
        reader.wait(i)
        here = stack[tokens:, at]
        stack_term = dot(stack[:, at], here, NT)
        error_term = dot(here, error_here[at, :])
        by_stack = stack_term if by_stack is None else by_stack + stack_term
        result = error_term if result is None else result + error_term
    gram[...] = by_stack[tokens:]
    own, oth = halves(og, half)
    by_acts = split3(by_stack[:tokens] * scale, axis=1)
    result += sum3(dot(by_acts[:half], own, TN) + dot(by_acts[half:], oth, TN))
    right[...] = result
    left_copy.wait()


def gram_schmidt(g):
    width = g.shape[0]
    rows = lax.broadcasted_iota(jnp.int32, (width, width), 0)
    columns = lax.broadcasted_iota(jnp.int32, (width, width), 1)
    coeffs = jnp.zeros((width, width), F32)
    products = jnp.zeros((width, width), F32)
    for k in range(width):
        along = products[k : k + 1]
        unit = (rows[:, :1] == k).astype(F32)
        v = unit - jnp.sum(along * coeffs, axis=1, keepdims=True)
        inner = g[:, k : k + 1] - jnp.sum(along * products, axis=1, keepdims=True)
        square = jnp.maximum(jnp.sum(v * inner, axis=0, keepdims=True), 0.0)
        inverse = lax.rsqrt(square + 1e-06)
        coeffs = jnp.where(columns == k, v * inverse, coeffs)
        products = jnp.where(columns == k, inner * inverse, products)
        yield coeffs


def right_sum_kernel(first, second, third, fourth, after, out, token):
    token[...] = jnp.zeros_like(token)
    out[...] = (first[...] + third[...]) + (second[...] + fourth[...])


def final_kernel(
    scale, inverse_replicas, first, second, third, fourth, metric, og, left_rows, momentum, after, acts, acts_oth, error,
    new_error, new_momentum, stack, rest, error_here, slots, sems, out_sems,
):
    tokens, cols = og.shape
    half, width = acts.shape
    rank = left_rows.shape[0]
    rows = blocks(width)
    reader = Reader(
        [
            [
                (acts.at[:, at], stack.at[:half, at]),
                (acts_oth.at[:, at], stack.at[half:tokens, at]),
                (error.at[at, :], error_here.at[at, :]),
            ]
            for at in rows
        ],
        sems,
    )
    for i in range(3):
        stack[tokens + i * rank : tokens + (i + 1) * rank, :] = left_rows[...]
    total = ((first[...] + third[...]) + (second[...] + fourth[...])) * (-inverse_replicas / scale)
    own, oth = halves(og, half)
    rest[:half] = own
    rest[half:tokens] = oth
    rest[tokens:] = split3(exact_dot(metric[...], total))
    writer = Writer(slots, out_sems)
    for i, at in enumerate(rows):
        reader.wait(i)
        product = dot(stack[:, at], rest[...], TN)
        writer.put((product * scale + error_here[at, :].astype(F32)).astype(BF16), new_error.at[at, :])
    count = momentum.shape[0]
    mine = pl.ds(pl.multiple_of(lax.axis_index("dp") * count, count), count)
    approx = dot(stack[tokens:, mine], rest[tokens:], TN) * -scale
    new_momentum[...] = (0.9 * momentum[...].astype(F32) + approx).astype(BF16)
    writer.finish()


def per_device(acts, out_grad, weight, error, momentum, q_init):
    tokens, cols = out_grad.shape
    half, width = acts.shape
    rank = q_init.shape[1]
    replicas = lax.axis_size("dp")
    scale = 1.0 / tokens**0.5
    swap = [(0, 1), (1, 0)]
    shape = jax.ShapeDtypeStruct
    side = 4

    def exchange(value, stride):
        def to(step):
            moved = lambda i: i + ((i // stride + step) % side - i // stride % side) * stride
            return [(i, moved(i)) for i in range(replicas)]

        return [value] + [lax.ppermute(value, "dp", to(step)) for step in range(1, side)]

    def right_sum(values, after):
        return call(
            right_sum_kernel,
            [VMEM] * (side + 1),
            [VMEM] * 2,
            [shape((rank, cols), F32), TOKEN],
            (*values, after),
            flops=side * rank * cols,
            moved=MIB // 4,
        )

    def input_own(part, after, *first_part):
        return call(
            functools.partial(input_own_kernel, part),
            [VMEM, HBM, VMEM, VMEM] + [HBM] * part,
            [HBM, VMEM],
            [pltpu.HBM((half, width), BF16), TOKEN],
            (out_grad, weight, received, after, *first_part),
            flops=tokens * cols * width // 2,
            moved=8 * MIB,
            scratch=[
                pltpu.VMEM((width, cols), BF16),
                pltpu.VMEM((4, half, BLOCK), BF16),
                dma((n_blocks, 1)),
                dma((4,)),
            ],
            aliases={4: 0} if part else {},
        )

    dma = pltpu.SemaphoreType.DMA
    n_blocks = width // BLOCK

    acts_oth = lax.ppermute(acts, "tensor", swap)

    part, pq_oth = call(
        functools.partial(left_own_kernel, scale),
        [HBM, HBM, HBM, HBM],
        [VMEM] * 2,
        [shape((rank, width), F32), shape((3 * rank, half), BF16)],
        (q_init.T, out_grad, acts, error),
        flops=2 * 96 * width * 768,
        moved=13 * MIB,
        scratch=[
            pltpu.VMEM((rank, cols), F32),
            pltpu.VMEM((tokens, cols), BF16),
            pltpu.VMEM((half, width), BF16),
            pltpu.VMEM((width, cols), BF16),
            dma((n_blocks, 2)),
            dma((2,)),
        ],
    )
    left_parts, acts_oth, left_done = call(
        left_kernel,
        [VMEM] * 3,
        [HBM, HBM, VMEM],
        [pltpu.HBM((replicas, rank, CHUNK), BF16), pltpu.HBM((half, width), BF16), TOKEN],
        (pq_oth, acts_oth, part),
        flops=2 * 96 * width * 256,
        moved=6 * MIB,
        scratch=[pltpu.VMEM((replicas, rank, CHUNK), BF16), dma((n_blocks + 1,))],
    )
    gathered = lax.all_to_all(left_parts, "dp", 0, 0, tiled=True)
    oth_input, oth_done = call(
        input_oth_kernel,
        [VMEM, HBM, VMEM],
        [HBM, VMEM],
        [pltpu.HBM((half, width), BF16), TOKEN],
        (out_grad, weight, left_done),
        flops=tokens * cols * width,
        moved=13 * MIB,
        scratch=[
            pltpu.VMEM((width, cols), BF16),
            pltpu.VMEM((4, half, BLOCK), BF16),
            dma((n_blocks, 1)),
            dma((4,)),
        ],
    )

    left_copies = call(
        left_sum_kernel,
        [VMEM, VMEM],
        VMEM,
        shape((replicas, rank, CHUNK), BF16),
        (gathered, oth_done),
        flops=replicas * rank * CHUNK,
        moved=MIB,
    )
    left = lax.all_to_all(left_copies, "dp", 0, 0, tiled=True)
    oth_input = call(
        pass_kernel,
        [HBM, VMEM],
        HBM,
        pltpu.HBM((half, width), BF16),
        (oth_input, left),
        flops=1,
        moved=4096,
        aliases={0: 0},
    )
    received = lax.ppermute(oth_input, "tensor", swap)

    right, gram, left_rows = call(
        functools.partial(right_kernel, scale),
        [VMEM, VMEM, HBM, HBM, HBM],
        [VMEM, VMEM, HBM],
        [shape((rank, cols), F32), shape((rank, rank), F32), pltpu.HBM((rank, width), BF16)],
        (out_grad, left, acts, acts_oth, error),
        flops=2 * rank * width * 1024,
        moved=17 * MIB,
        scratch=[pltpu.VMEM((tokens + rank, width), BF16), pltpu.VMEM((width, cols), BF16), dma((2 * n_blocks, 3)), dma((1,))],
    )
    rows = exchange(right, 1)
    metric = call(
        gram_schmidt_kernel, [VMEM], VMEM, shape((rank, rank), F32), (gram,), flops=MIB * 1024, moved=8192
    )
    right, right_done = right_sum(rows, metric)
    rows = exchange(right, side)
    input_grad, input_done = input_own(0, right_done)
    right, right_done = right_sum(rows, input_done)
    rows = exchange(right, side * side)
    input_grad, input_done = input_own(1, right_done, input_grad)
    new_error, new_momentum = call(
        functools.partial(final_kernel, scale, 1.0 / replicas),
        [VMEM] * (side + 5) + [HBM] * 3,
        [HBM, VMEM],
        [pltpu.HBM((width, cols), BF16), shape(momentum.shape, BF16)],
        (*rows, metric, out_grad, left_rows, momentum, input_done, acts, acts_oth, error),
        flops=2 * (tokens + 3 * rank) * width * cols,
        moved=25 * MIB,
        scratch=[
            pltpu.VMEM((tokens + 3 * rank, width), BF16),
            pltpu.VMEM((tokens + 3 * rank, cols), BF16),
            pltpu.VMEM((width, cols), BF16),
            pltpu.VMEM((4, BLOCK, cols), BF16),
            dma((n_blocks, 3)),
            dma((4,)),
        ],
    )
    return (new_error, new_momentum, input_grad)


def solution(mesh):
    return jax.shard_map(
        per_device,
        mesh=mesh,
        in_specs=(
            P(("dp", "tensor"), None),
            P("dp", "tensor"),
            P(None, "tensor"),
            P("dp", "tensor"),
            P("dp", "tensor"),
            P("tensor", None),
        ),
        out_specs=(P("dp", "tensor"), P("dp", "tensor"), P(("dp", "tensor"), None)),
        check_vma=False,
    )
```

```python
import functools

import jax
import jax.numpy as jnp
from jax import lax
from jax.experimental import pallas as pl
from jax.experimental.pallas import tpu as pltpu
from jax.sharding import PartitionSpec as P

F32 = jnp.float32
BF16 = jnp.bfloat16
MIB = 1024 * 1024
BLOCK = 1024
CHUNK = 128

NN = (((1,), (0,)), ((), ()))
NT = (((1,), (1,)), ((), ()))
TN = (((0,), (0,)), ((), ()))

VMEM = pl.BlockSpec(memory_space=pltpu.VMEM)
HBM = pl.BlockSpec(memory_space=pltpu.HBM)
TOKEN = jax.ShapeDtypeStruct((8, 128), jnp.float32)


def in_hbm(x):
    return pltpu.with_memory_space_constraint(x, pltpu.HBM)


def dot(a, b, dims=NN):
    return lax.dot_general(a, b, dims, preferred_element_type=F32)


def exact_dot(a, b, dims=NN):
    return lax.dot_general(a, b, dims, precision=lax.Precision.HIGHEST, preferred_element_type=F32)


def split3(x, axis=0):
    high = x.astype(BF16)
    rest = x - high.astype(F32)
    middle = rest.astype(BF16)
    low = (rest - middle.astype(F32)).astype(BF16)
    return jnp.concatenate([high, middle, low], axis=axis)


def split2(x):
    high = x.astype(BF16)
    return jnp.concatenate([high, (x - high.astype(F32)).astype(BF16)], axis=0)


def sum2(x):
    rows = x.shape[0] // 2
    return x[:rows] + x[rows:]


def sum3(x):
    rows = x.shape[0] // 3
    return x[:rows] + x[rows : 2 * rows] + x[2 * rows :]


def call(kernel, in_specs, out_specs, out_shape, args, flops, moved, scratch=(), aliases={}):
    args = [in_hbm(x) if spec is HBM else x for spec, x in zip(in_specs, args)]
    return pl.pallas_call(
        kernel,
        in_specs=in_specs,
        out_specs=out_specs,
        out_shape=out_shape,
        scratch_shapes=list(scratch),
        input_output_aliases=aliases,
        compiler_params=pltpu.CompilerParams(vmem_limit_bytes=32 * MIB),
        cost_estimate=pl.CostEstimate(flops=flops, bytes_accessed=moved, transcendentals=0),
    )(*args)


def halves(og, half):
    core = lax.axis_index("tensor")
    own = pl.multiple_of(core * half, half)
    oth = pl.multiple_of((1 - core) * half, half)
    return og[pl.ds(own, half), :], og[pl.ds(oth, half), :]


def blocks(width, size=BLOCK):
    return [slice(i, i + size) for i in range(0, width, size)]


class Reader:
    def __init__(self, pairs, sems, ahead=3):
        self.ahead = ahead
        self.copies = [
            [pltpu.make_async_copy(source, target, sems.at[i, j]) for j, (source, target) in enumerate(block)]
            for i, block in enumerate(pairs)
        ]
        for block in self.copies[: self.ahead]:
            for copy in block:
                copy.start()

    def wait(self, i):
        if i + self.ahead < len(self.copies):
            for copy in self.copies[i + self.ahead]:
                copy.start()
        for copy in self.copies[i]:
            copy.wait()


class Writer:
    def __init__(self, slots, sems):
        self.slots, self.sems, self.copies = slots, sems, []

    def put(self, value, target):
        at = len(self.copies)
        slot = at % self.slots.shape[0]
        if at >= self.slots.shape[0]:
            self.copies[at - self.slots.shape[0]].wait()
        rows = value.shape[0]
        self.slots[slot, :rows] = value
        copy = pltpu.make_async_copy(self.slots.at[slot, :rows], target, self.sems.at[slot])
        copy.start()
        self.copies.append(copy)

    def finish(self):
        for copy in self.copies[-self.slots.shape[0] :]:
            copy.wait()


def left_own_kernel(
    scale, q_hbm, og_hbm, acts, error, part, pq_oth, q, og, acts_here, error_here, sems, small_sems
):
    half, width = acts.shape
    rows = blocks(BLOCK, BLOCK // 2) + blocks(width)[1:]
    q_copy = pltpu.make_async_copy(q_hbm, q, small_sems.at[0])
    og_copy = pltpu.make_async_copy(og_hbm, og, small_sems.at[1])
    q_copy.start()
    reads = [[(error.at[at, :], error_here.at[at, :]), (acts.at[:, at], acts_here.at[:, at])] for at in rows]
    reader = Reader(reads, sems, ahead=2)
    og_copy.start()
    q_copy.wait()
    q2 = split2(q[...])
    for i, at in enumerate(rows):
        reader.wait(i)
        by_error = sum2(dot(error_here[at, :], q2, NT).T)
        if i == 0:
            og_copy.wait()
            og_own, og_oth = halves(og, half)
            pq2 = split2(sum2(dot(q2, og_own, NT)) * scale)
            pq_oth[...] = split2(sum2(dot(q2, og_oth, NT)) * scale)
        part[:, at] = by_error + sum2(dot(pq2, acts_here[:, at]))


def left_kernel(pq2, acts, part, left, acts_kept, token, here, sems):
    token[...] = jnp.zeros_like(token)
    rows = blocks(acts.shape[1])
    copies = [pltpu.make_async_copy(acts, acts_kept, sems.at[len(rows)])]
    copies[0].start()
    for i, at in enumerate(rows):
        total = part[:, at] + sum2(dot(pq2[...], acts[:, at]))
        count = BLOCK // CHUNK
        chunks = slice(i * count, (i + 1) * count)
        for j in range(count):
            here[i * count + j] = total[:, j * CHUNK : (j + 1) * CHUNK].astype(BF16)
        copies.append(pltpu.make_async_copy(here.at[chunks], left.at[chunks], sems.at[i]))
        copies[-1].start()
    for copy in copies:
        copy.wait()


def input_oth_kernel(og, weight, after, part, token, weight_here, slots, sems, out_sems):
    token[...] = jnp.zeros_like(token)
    half, width = part.shape
    rows = blocks(width)
    reader = Reader([[(weight.at[at, :], weight_here.at[at, :])] for at in rows], sems)
    _, oth = halves(og, half)
    writer = Writer(slots, out_sems)
    for i, at in enumerate(rows):
        reader.wait(i)
        writer.put(dot(oth, weight_here[at, :], NT).astype(BF16), part.at[:, at])
    writer.finish()


def pass_kernel(part, after, out):
    pass


def input_own_kernel(part, og, weight, received, after, *refs):
    ahead = []
    if part == 0:
        out, token, weight_here, slots, sems, out_sems = refs
    else:
        _, acts, acts_oth, error, out, token, stack, first_error, weight_here, slots, sems, out_sems, ahead_sems = refs
        pairs = [
            (acts.at[:, :BLOCK], stack.at[: acts.shape[0], :]),
            (acts_oth.at[:, :BLOCK], stack.at[acts.shape[0] :, :]),
            (error.at[:BLOCK, :], first_error),
        ]
        ahead = [pltpu.make_async_copy(source, target, ahead_sems.at[i]) for i, (source, target) in enumerate(pairs)]
    token[...] = jnp.zeros_like(token)
    half, width = received.shape
    rows = blocks(width)
    rows = rows[: len(rows) // 2] if part == 0 else rows[len(rows) // 2 :]
    reader = Reader([[(weight.at[at, :], weight_here.at[at, :])] for at in rows], sems)
    for copy in ahead:
        copy.start()
    own, _ = halves(og, half)
    writer = Writer(slots, out_sems)
    for i, at in enumerate(rows):
        reader.wait(i)
        product = dot(own, weight_here[at, :], NT).astype(BF16)
        writer.put((product.astype(F32) + received[:, at].astype(F32)).astype(BF16), out.at[:, at])
    writer.finish()
    for copy in ahead:
        copy.wait()


def gram_schmidt_kernel(gram, metric):
    for coeffs in gram_schmidt(gram[...]):
        pass
    metric[...] = exact_dot(coeffs, coeffs, NT)


def left_sum_kernel(parts, after, out):
    total = jnp.sum(parts[...].astype(F32), axis=0).astype(BF16)
    out[...] = jnp.broadcast_to(total[None], out.shape)


def right_kernel(
    scale, og, left, acts, acts_oth, error, right, gram, left_rows, stack, error_here, sems, out_sems
):
    tokens, cols = og.shape
    half, width = acts.shape
    rows = blocks(width, BLOCK // 2)
    reader = Reader(
        [
            [
                (acts.at[:, at], stack.at[:half, at]),
                (acts_oth.at[:, at], stack.at[half:tokens, at]),
                (error.at[at, :], error_here.at[at, :]),
            ]
            for at in rows
        ],
        sems,
        ahead=8,
    )
    for i in range(left.shape[0]):
        stack[tokens:, i * CHUNK : (i + 1) * CHUNK] = left[i]
    left_copy = pltpu.make_async_copy(stack.at[tokens:, :], left_rows, out_sems.at[0])
    left_copy.start()
    by_stack, result = None, None
    for i, at in enumerate(rows):
        reader.wait(i)
        here = stack[tokens:, at]
        stack_term = dot(stack[:, at], here, NT)
        error_term = dot(here, error_here[at, :])
        by_stack = stack_term if by_stack is None else by_stack + stack_term
        result = error_term if result is None else result + error_term
    gram[...] = by_stack[tokens:]
    own, oth = halves(og, half)
    by_acts = split3(by_stack[:tokens] * scale, axis=1)
    result += sum3(dot(by_acts[:half], own, TN) + dot(by_acts[half:], oth, TN))
    right[...] = result
    left_copy.wait()


def gram_schmidt(g):
    width = g.shape[0]
    rows = lax.broadcasted_iota(jnp.int32, (width, width), 0)
    columns = lax.broadcasted_iota(jnp.int32, (width, width), 1)
    coeffs = jnp.zeros((width, width), F32)
    products = jnp.zeros((width, width), F32)
    for k in range(width):
        along = products[k : k + 1]
        unit = (rows[:, :1] == k).astype(F32)
        v = unit - jnp.sum(along * coeffs, axis=1, keepdims=True)
        inner = g[:, k : k + 1] - jnp.sum(along * products, axis=1, keepdims=True)
        square = jnp.maximum(jnp.sum(v * inner, axis=0, keepdims=True), 0.0)
        inverse = lax.rsqrt(square + 1e-06)
        coeffs = jnp.where(columns == k, v * inverse, coeffs)
        products = jnp.where(columns == k, inner * inverse, products)
        yield coeffs


def right_sum_kernel(first, second, third, fourth, after, out, token):
    token[...] = jnp.zeros_like(token)
    out[...] = (first[...] + third[...]) + (second[...] + fourth[...])


def final_kernel(
    scale, inverse_replicas, first, second, third, fourth, metric, og, left_rows, momentum, first_stack, first_error, acts, acts_oth, error,
    new_error, new_momentum, stack, rest, error_here, slots, sems, out_sems,
):
    tokens, cols = og.shape
    half, width = acts.shape
    rank = left_rows.shape[0]
    rows = blocks(width)
    reader = Reader(
        [
            [
                (acts.at[:, at], stack.at[:half, at]),
                (acts_oth.at[:, at], stack.at[half:tokens, at]),
                (error.at[at, :], error_here.at[at, :]),
            ]
            for at in rows[1:]
        ],
        sems,
    )
    for i in range(3):
        stack[tokens + i * rank : tokens + (i + 1) * rank, :] = left_rows[...]
    total = ((first[...] + third[...]) + (second[...] + fourth[...])) * (-inverse_replicas / scale)
    own, oth = halves(og, half)
    rest[:half] = own
    rest[half:tokens] = oth
    rest[tokens:] = split3(exact_dot(metric[...], total))
    writer = Writer(slots, out_sems)
    for i, at in enumerate(rows):
        if i == 0:
            product = dot(first_stack[...], rest[:tokens], TN) + dot(stack[tokens:, at], rest[tokens:], TN)
            base = first_error[...]
        else:
            reader.wait(i - 1)
            product = dot(stack[:, at], rest[...], TN)
            base = error_here[at, :]
        writer.put((product * scale + base.astype(F32)).astype(BF16), new_error.at[at, :])
    count = momentum.shape[0]
    mine = pl.ds(pl.multiple_of(lax.axis_index("dp") * count, count), count)
    approx = dot(stack[tokens:, mine], rest[tokens:], TN) * -scale
    new_momentum[...] = (0.9 * momentum[...].astype(F32) + approx).astype(BF16)
    writer.finish()


def per_device(acts, out_grad, weight, error, momentum, q_init):
    tokens, cols = out_grad.shape
    half, width = acts.shape
    rank = q_init.shape[1]
    replicas = lax.axis_size("dp")
    scale = 1.0 / tokens**0.5
    swap = [(0, 1), (1, 0)]
    shape = jax.ShapeDtypeStruct
    side = 4

    def exchange(value, stride):
        def to(step):
            moved = lambda i: i + ((i // stride + step) % side - i // stride % side) * stride
            return [(i, moved(i)) for i in range(replicas)]

        return [value] + [lax.ppermute(value, "dp", to(step)) for step in range(1, side)]

    def right_sum(values, after):
        return call(
            right_sum_kernel,
            [VMEM] * (side + 1),
            [VMEM] * 2,
            [shape((rank, cols), F32), TOKEN],
            (*values, after),
            flops=side * rank * cols,
            moved=MIB // 4,
        )

    def input_own(part, after, *more):
        return call(
            functools.partial(input_own_kernel, part),
            [VMEM, HBM, VMEM, VMEM] + [HBM] * len(more),
            [HBM, VMEM] + [VMEM] * (2 * part),
            [pltpu.HBM((half, width), BF16), TOKEN]
            + [shape((tokens, BLOCK), BF16), shape((BLOCK, cols), BF16)] * part,
            (out_grad, weight, received, after, *more),
            flops=tokens * cols * width // 2,
            moved=8 * MIB,
            scratch=[
                pltpu.VMEM((width, cols), BF16),
                pltpu.VMEM((4, half, BLOCK), BF16),
                dma((n_blocks, 1)),
                dma((4,)),
            ]
            + [dma((3,))] * part,
            aliases={4: 0} if part else {},
        )

    dma = pltpu.SemaphoreType.DMA
    n_blocks = width // BLOCK

    acts_oth = lax.ppermute(acts, "tensor", swap)

    part, pq_oth = call(
        functools.partial(left_own_kernel, scale),
        [HBM, HBM, HBM, HBM],
        [VMEM] * 2,
        [shape((rank, width), F32), shape((2 * rank, half), BF16)],
        (q_init.T, out_grad, acts, error),
        flops=2 * 96 * width * 768,
        moved=13 * MIB,
        scratch=[
            pltpu.VMEM((rank, cols), F32),
            pltpu.VMEM((tokens, cols), BF16),
            pltpu.VMEM((half, width), BF16),
            pltpu.VMEM((width, cols), BF16),
            dma((n_blocks + 1, 2)),
            dma((2,)),
        ],
    )
    left_parts, acts_oth, left_done = call(
        left_kernel,
        [VMEM] * 3,
        [HBM, HBM, VMEM],
        [pltpu.HBM((replicas, rank, CHUNK), BF16), pltpu.HBM((half, width), BF16), TOKEN],
        (pq_oth, acts_oth, part),
        flops=2 * 96 * width * 256,
        moved=6 * MIB,
        scratch=[pltpu.VMEM((replicas, rank, CHUNK), BF16), dma((n_blocks + 1,))],
    )
    gathered = lax.all_to_all(left_parts, "dp", 0, 0, tiled=True)
    oth_input, oth_done = call(
        input_oth_kernel,
        [VMEM, HBM, VMEM],
        [HBM, VMEM],
        [pltpu.HBM((half, width), BF16), TOKEN],
        (out_grad, weight, left_done),
        flops=tokens * cols * width,
        moved=13 * MIB,
        scratch=[
            pltpu.VMEM((width, cols), BF16),
            pltpu.VMEM((4, half, BLOCK), BF16),
            dma((n_blocks, 1)),
            dma((4,)),
        ],
    )

    left_copies = call(
        left_sum_kernel,
        [VMEM, VMEM],
        VMEM,
        shape((replicas, rank, CHUNK), BF16),
        (gathered, oth_done),
        flops=replicas * rank * CHUNK,
        moved=MIB,
    )
    left = lax.all_to_all(left_copies, "dp", 0, 0, tiled=True)
    oth_input = call(
        pass_kernel,
        [HBM, VMEM],
        HBM,
        pltpu.HBM((half, width), BF16),
        (oth_input, left),
        flops=1,
        moved=4096,
        aliases={0: 0},
    )
    received = lax.ppermute(oth_input, "tensor", swap)

    right, gram, left_rows = call(
        functools.partial(right_kernel, scale),
        [VMEM, VMEM, HBM, HBM, HBM],
        [VMEM, VMEM, HBM],
        [shape((rank, cols), F32), shape((rank, rank), F32), pltpu.HBM((rank, width), BF16)],
        (out_grad, left, acts, acts_oth, error),
        flops=2 * rank * width * 1024,
        moved=17 * MIB,
        scratch=[pltpu.VMEM((tokens + rank, width), BF16), pltpu.VMEM((width, cols), BF16), dma((2 * n_blocks, 3)), dma((1,))],
    )
    rows = exchange(right, 1)
    metric = call(
        gram_schmidt_kernel, [VMEM], VMEM, shape((rank, rank), F32), (gram,), flops=MIB * 1024, moved=8192
    )
    right, right_done = right_sum(rows, metric)
    rows = exchange(right, side)
    input_grad, input_done = input_own(0, right_done)
    right, right_done = right_sum(rows, input_done)
    rows = exchange(right, side * side)
    input_grad, _, first_stack, first_error = input_own(1, right_done, input_grad, acts, acts_oth, error)
    new_error, new_momentum = call(
        functools.partial(final_kernel, scale, 1.0 / replicas),
        [VMEM] * (side + 6) + [HBM] * 3,
        [HBM, VMEM],
        [pltpu.HBM((width, cols), BF16), shape(momentum.shape, BF16)],
        (*rows, metric, out_grad, left_rows, momentum, first_stack, first_error, acts, acts_oth, error),
        flops=2 * (tokens + 3 * rank) * width * cols,
        moved=25 * MIB,
        scratch=[
            pltpu.VMEM((tokens + 3 * rank, width), BF16),
            pltpu.VMEM((tokens + 3 * rank, cols), BF16),
            pltpu.VMEM((width, cols), BF16),
            pltpu.VMEM((4, BLOCK, cols), BF16),
            dma((n_blocks, 3)),
            dma((4,)),
        ],
    )
    return (new_error, new_momentum, input_grad)


def solution(mesh):
    return jax.shard_map(
        per_device,
        mesh=mesh,
        in_specs=(
            P(("dp", "tensor"), None),
            P("dp", "tensor"),
            P(None, "tensor"),
            P("dp", "tensor"),
            P("dp", "tensor"),
            P("tensor", None),
        ),
        out_specs=(P("dp", "tensor"), P("dp", "tensor"), P(("dp", "tensor"), None)),
        check_vma=False,
    )
```

```python
import functools

import jax
import jax.numpy as jnp
from jax import lax
from jax.experimental import pallas as pl
from jax.experimental.pallas import tpu as pltpu
from jax.sharding import PartitionSpec as P

F32 = jnp.float32
BF16 = jnp.bfloat16
MIB = 1024 * 1024
BLOCK = 1024
CHUNK = 128

NN = (((1,), (0,)), ((), ()))
NT = (((1,), (1,)), ((), ()))
TN = (((0,), (0,)), ((), ()))

VMEM = pl.BlockSpec(memory_space=pltpu.VMEM)
HBM = pl.BlockSpec(memory_space=pltpu.HBM)
TOKEN = jax.ShapeDtypeStruct((8, 128), jnp.float32)


def in_hbm(x):
    return pltpu.with_memory_space_constraint(x, pltpu.HBM)


def dot(a, b, dims=NN):
    return lax.dot_general(a, b, dims, preferred_element_type=F32)


def exact_dot(a, b, dims=NN):
    return lax.dot_general(a, b, dims, precision=lax.Precision.HIGHEST, preferred_element_type=F32)


def split3(x, axis=0):
    high = x.astype(BF16)
    rest = x - high.astype(F32)
    middle = rest.astype(BF16)
    low = (rest - middle.astype(F32)).astype(BF16)
    return jnp.concatenate([high, middle, low], axis=axis)


def split2(x):
    high = x.astype(BF16)
    return jnp.concatenate([high, (x - high.astype(F32)).astype(BF16)], axis=0)


def sum2(x):
    rows = x.shape[0] // 2
    return x[:rows] + x[rows:]


def sum3(x):
    rows = x.shape[0] // 3
    return x[:rows] + x[rows : 2 * rows] + x[2 * rows :]


def call(kernel, in_specs, out_specs, out_shape, args, flops, moved, scratch=(), aliases={}):
    args = [in_hbm(x) if spec is HBM else x for spec, x in zip(in_specs, args)]
    return pl.pallas_call(
        kernel,
        in_specs=in_specs,
        out_specs=out_specs,
        out_shape=out_shape,
        scratch_shapes=list(scratch),
        input_output_aliases=aliases,
        compiler_params=pltpu.CompilerParams(vmem_limit_bytes=32 * MIB),
        cost_estimate=pl.CostEstimate(flops=flops, bytes_accessed=moved, transcendentals=0),
    )(*args)


def halves(og, half):
    core = lax.axis_index("tensor")
    own = pl.multiple_of(core * half, half)
    oth = pl.multiple_of((1 - core) * half, half)
    return og[pl.ds(own, half), :], og[pl.ds(oth, half), :]


def blocks(width, size=BLOCK):
    return [slice(i, i + size) for i in range(0, width, size)]


class Reader:
    def __init__(self, pairs, sems, ahead=3):
        self.ahead = ahead
        self.copies = [
            [pltpu.make_async_copy(source, target, sems.at[i, j]) for j, (source, target) in enumerate(block)]
            for i, block in enumerate(pairs)
        ]
        for block in self.copies[: self.ahead]:
            for copy in block:
                copy.start()

    def wait(self, i):
        if i + self.ahead < len(self.copies):
            for copy in self.copies[i + self.ahead]:
                copy.start()
        for copy in self.copies[i]:
            copy.wait()


class Writer:
    def __init__(self, slots, sems):
        self.slots, self.sems, self.copies = slots, sems, []

    def put(self, value, target):
        at = len(self.copies)
        slot = at % self.slots.shape[0]
        if at >= self.slots.shape[0]:
            self.copies[at - self.slots.shape[0]].wait()
        rows = value.shape[0]
        self.slots[slot, :rows] = value
        copy = pltpu.make_async_copy(self.slots.at[slot, :rows], target, self.sems.at[slot])
        copy.start()
        self.copies.append(copy)

    def finish(self):
        for copy in self.copies[-self.slots.shape[0] :]:
            copy.wait()


def left_own_kernel(
    scale, q_hbm, og_hbm, acts, error, part, pq_oth, q, og, acts_here, error_here, sems, small_sems
):
    half, width = acts.shape
    rows = blocks(BLOCK, BLOCK // 2) + blocks(width)[1:]
    q_copy = pltpu.make_async_copy(q_hbm, q, small_sems.at[0])
    og_copy = pltpu.make_async_copy(og_hbm, og, small_sems.at[1])
    q_copy.start()
    reads = [[(error.at[at, :], error_here.at[at, :]), (acts.at[:, at], acts_here.at[:, at])] for at in rows]
    reader = Reader(reads, sems, ahead=2)
    og_copy.start()
    q_copy.wait()
    q2 = split2(q[...])
    for i, at in enumerate(rows):
        reader.wait(i)
        by_error = sum2(dot(error_here[at, :], q2, NT).T)
        if i == 0:
            og_copy.wait()
            og_own, og_oth = halves(og, half)
            pq2 = split2(sum2(dot(q2, og_own, NT)) * scale)
            pq_oth[...] = split2(sum2(dot(q2, og_oth, NT)) * scale)
        part[:, at] = by_error + sum2(dot(pq2, acts_here[:, at]))


def left_kernel(pq2, acts, part, left, acts_kept, token, here, sems):
    token[...] = jnp.zeros_like(token)
    rows = blocks(acts.shape[1])
    copies = [pltpu.make_async_copy(acts, acts_kept, sems.at[len(rows)])]
    copies[0].start()
    for i, at in enumerate(rows):
        total = part[:, at] + sum2(dot(pq2[...], acts[:, at]))
        count = BLOCK // CHUNK
        chunks = slice(i * count, (i + 1) * count)
        for j in range(count):
            here[i * count + j] = total[:, j * CHUNK : (j + 1) * CHUNK].astype(BF16)
        copies.append(pltpu.make_async_copy(here.at[chunks], left.at[chunks], sems.at[i]))
        copies[-1].start()
    for copy in copies:
        copy.wait()


def input_oth_kernel(og, weight, after, part, token, weight_here, slots, sems, out_sems):
    token[...] = jnp.zeros_like(token)
    half, width = part.shape
    rows = blocks(width)
    reader = Reader([[(weight.at[at, :], weight_here.at[at, :])] for at in rows], sems)
    _, oth = halves(og, half)
    writer = Writer(slots, out_sems)
    for i, at in enumerate(rows):
        reader.wait(i)
        writer.put(dot(oth, weight_here[at, :], NT).astype(BF16), part.at[:, at])
    writer.finish()


def pass_kernel(part, after, out):
    pass


def input_own_kernel(part, og, weight, received, after, *refs):
    ahead = []
    if part == 0:
        gram, coeffs, products, out, token, metric, weight_here, slots, sems, out_sems = refs
    else:
        _, acts, acts_oth, error, out, token, stack, first_error, weight_here, slots, sems, out_sems, ahead_sems = refs
        pairs = [
            (acts.at[:, :BLOCK], stack.at[: acts.shape[0], :]),
            (acts_oth.at[:, :BLOCK], stack.at[acts.shape[0] :, :]),
            (error.at[:BLOCK, :], first_error),
        ]
        ahead = [pltpu.make_async_copy(source, target, ahead_sems.at[i]) for i, (source, target) in enumerate(pairs)]
    token[...] = jnp.zeros_like(token)
    half, width = received.shape
    rows = blocks(width)
    rows = rows[: len(rows) // 2] if part == 0 else rows[len(rows) // 2 :]
    reader = Reader([[(weight.at[at, :], weight_here.at[at, :])] for at in rows], sems)
    for copy in ahead:
        copy.start()
    own, _ = halves(og, half)
    if part == 0:
        rank = gram.shape[0]
        full, _ = gram_schmidt(gram[...], range(rank * 3 // 4, rank), coeffs[...], products[...])
        metric[...] = exact_dot(full, full, NT)
    writer = Writer(slots, out_sems)
    for i, at in enumerate(rows):
        reader.wait(i)
        product = dot(own, weight_here[at, :], NT).astype(BF16)
        writer.put((product.astype(F32) + received[:, at].astype(F32)).astype(BF16), out.at[:, at])
    writer.finish()
    for copy in ahead:
        copy.wait()


def gram_schmidt_kernel(gram, coeffs, products):
    zeros = jnp.zeros(gram.shape, F32)
    coeffs[...], products[...] = gram_schmidt(gram[...], range(gram.shape[0] * 3 // 4), zeros, zeros)


def left_sum_kernel(parts, after, out):
    total = jnp.sum(parts[...].astype(F32), axis=0).astype(BF16)
    out[...] = jnp.broadcast_to(total[None], out.shape)


def right_kernel(
    scale, og, left, acts, acts_oth, error, right, gram, left_rows, stack, error_here, sems, out_sems
):
    tokens, cols = og.shape
    half, width = acts.shape
    rows = blocks(width, BLOCK // 2)
    reader = Reader(
        [
            [
                (acts.at[:, at], stack.at[:half, at]),
                (acts_oth.at[:, at], stack.at[half:tokens, at]),
                (error.at[at, :], error_here.at[at, :]),
            ]
            for at in rows
        ],
        sems,
        ahead=8,
    )
    for i in range(left.shape[0]):
        stack[tokens:, i * CHUNK : (i + 1) * CHUNK] = left[i]
    left_copy = pltpu.make_async_copy(stack.at[tokens:, :], left_rows, out_sems.at[0])
    left_copy.start()
    by_stack, result = None, None
    for i, at in enumerate(rows):
        reader.wait(i)
        here = stack[tokens:, at]
        stack_term = dot(stack[:, at], here, NT)
        error_term = dot(here, error_here[at, :])
        by_stack = stack_term if by_stack is None else by_stack + stack_term
        result = error_term if result is None else result + error_term
    gram[...] = by_stack[tokens:]
    own, oth = halves(og, half)
    by_acts = split3(by_stack[:tokens] * scale, axis=1)
    result += sum3(dot(by_acts[:half], own, TN) + dot(by_acts[half:], oth, TN))
    right[...] = result
    left_copy.wait()


def gram_schmidt(g, steps, coeffs, products):
    width = g.shape[0]
    rows = lax.broadcasted_iota(jnp.int32, (width, width), 0)
    columns = lax.broadcasted_iota(jnp.int32, (width, width), 1)
    for k in steps:
        along = products[k : k + 1]
        unit = (rows[:, :1] == k).astype(F32)
        v = unit - jnp.sum(along * coeffs, axis=1, keepdims=True)
        inner = g[:, k : k + 1] - jnp.sum(along * products, axis=1, keepdims=True)
        square = jnp.maximum(jnp.sum(v * inner, axis=0, keepdims=True), 0.0)
        inverse = lax.rsqrt(square + 1e-06)
        coeffs = jnp.where(columns == k, v * inverse, coeffs)
        products = jnp.where(columns == k, inner * inverse, products)
    return coeffs, products


def right_sum_kernel(first, second, third, fourth, after, out, token):
    token[...] = jnp.zeros_like(token)
    out[...] = (first[...] + third[...]) + (second[...] + fourth[...])


def final_kernel(
    scale, inverse_replicas, first, second, third, fourth, metric, og, left_rows, momentum, first_stack, first_error, acts, acts_oth, error,
    new_error, new_momentum, stack, rest, error_here, slots, sems, out_sems,
):
    tokens, cols = og.shape
    half, width = acts.shape
    rank = left_rows.shape[0]
    rows = blocks(width)
    reader = Reader(
        [
            [
                (acts.at[:, at], stack.at[:half, at]),
                (acts_oth.at[:, at], stack.at[half:tokens, at]),
                (error.at[at, :], error_here.at[at, :]),
            ]
            for at in rows[1:]
        ],
        sems,
    )
    for i in range(3):
        stack[tokens + i * rank : tokens + (i + 1) * rank, :] = left_rows[...]
    total = ((first[...] + third[...]) + (second[...] + fourth[...])) * (-inverse_replicas / scale)
    own, oth = halves(og, half)
    rest[:half] = own
    rest[half:tokens] = oth
    rest[tokens:] = split3(exact_dot(metric[...], total))
    writer = Writer(slots, out_sems)
    for i, at in enumerate(rows):
        if i == 0:
            product = dot(first_stack[...], rest[:tokens], TN) + dot(stack[tokens:, at], rest[tokens:], TN)
            base = first_error[...]
        else:
            reader.wait(i - 1)
            product = dot(stack[:, at], rest[...], TN)
            base = error_here[at, :]
        writer.put((product * scale + base.astype(F32)).astype(BF16), new_error.at[at, :])
    count = momentum.shape[0]
    mine = pl.ds(pl.multiple_of(lax.axis_index("dp") * count, count), count)
    approx = dot(stack[tokens:, mine], rest[tokens:], TN) * -scale
    new_momentum[...] = (0.9 * momentum[...].astype(F32) + approx).astype(BF16)
    writer.finish()


def per_device(acts, out_grad, weight, error, momentum, q_init):
    tokens, cols = out_grad.shape
    half, width = acts.shape
    rank = q_init.shape[1]
    replicas = lax.axis_size("dp")
    scale = 1.0 / tokens**0.5
    swap = [(0, 1), (1, 0)]
    shape = jax.ShapeDtypeStruct
    side = 4

    def exchange(value, stride):
        def to(step):
            moved = lambda i: i + ((i // stride + step) % side - i // stride % side) * stride
            return [(i, moved(i)) for i in range(replicas)]

        return [value] + [lax.ppermute(value, "dp", to(step)) for step in range(1, side)]

    def right_sum(values, after):
        return call(
            right_sum_kernel,
            [VMEM] * (side + 1),
            [VMEM] * 2,
            [shape((rank, cols), F32), TOKEN],
            (*values, after),
            flops=side * rank * cols,
            moved=MIB // 4,
        )

    def input_own(part, after, *more):
        return call(
            functools.partial(input_own_kernel, part),
            [VMEM, HBM, VMEM, VMEM] + [HBM if part else VMEM] * len(more),
            [HBM, VMEM] + [VMEM] * (1 + part),
            [pltpu.HBM((half, width), BF16), TOKEN]
            + ([shape((tokens, BLOCK), BF16), shape((BLOCK, cols), BF16)] if part else [shape((rank, rank), F32)]),
            (out_grad, weight, received, after, *more),
            flops=tokens * cols * width // 2,
            moved=8 * MIB,
            scratch=[
                pltpu.VMEM((width, cols), BF16),
                pltpu.VMEM((4, half, BLOCK), BF16),
                dma((n_blocks, 1)),
                dma((4,)),
            ]
            + [dma((3,))] * part,
            aliases={4: 0} if part else {},
        )

    dma = pltpu.SemaphoreType.DMA
    n_blocks = width // BLOCK

    acts_oth = lax.ppermute(acts, "tensor", swap)

    part, pq_oth = call(
        functools.partial(left_own_kernel, scale),
        [HBM, HBM, HBM, HBM],
        [VMEM] * 2,
        [shape((rank, width), F32), shape((2 * rank, half), BF16)],
        (q_init.T, out_grad, acts, error),
        flops=2 * 96 * width * 768,
        moved=13 * MIB,
        scratch=[
            pltpu.VMEM((rank, cols), F32),
            pltpu.VMEM((tokens, cols), BF16),
            pltpu.VMEM((half, width), BF16),
            pltpu.VMEM((width, cols), BF16),
            dma((n_blocks + 1, 2)),
            dma((2,)),
        ],
    )
    left_parts, acts_oth, left_done = call(
        left_kernel,
        [VMEM] * 3,
        [HBM, HBM, VMEM],
        [pltpu.HBM((replicas, rank, CHUNK), BF16), pltpu.HBM((half, width), BF16), TOKEN],
        (pq_oth, acts_oth, part),
        flops=2 * 96 * width * 256,
        moved=6 * MIB,
        scratch=[pltpu.VMEM((replicas, rank, CHUNK), BF16), dma((n_blocks + 1,))],
    )
    gathered = lax.all_to_all(left_parts, "dp", 0, 0, tiled=True)
    oth_input, oth_done = call(
        input_oth_kernel,
        [VMEM, HBM, VMEM],
        [HBM, VMEM],
        [pltpu.HBM((half, width), BF16), TOKEN],
        (out_grad, weight, left_done),
        flops=tokens * cols * width,
        moved=13 * MIB,
        scratch=[
            pltpu.VMEM((width, cols), BF16),
            pltpu.VMEM((4, half, BLOCK), BF16),
            dma((n_blocks, 1)),
            dma((4,)),
        ],
    )

    left_copies = call(
        left_sum_kernel,
        [VMEM, VMEM],
        VMEM,
        shape((replicas, rank, CHUNK), BF16),
        (gathered, oth_done),
        flops=replicas * rank * CHUNK,
        moved=MIB,
    )
    left = lax.all_to_all(left_copies, "dp", 0, 0, tiled=True)
    oth_input = call(
        pass_kernel,
        [HBM, VMEM],
        HBM,
        pltpu.HBM((half, width), BF16),
        (oth_input, left),
        flops=1,
        moved=4096,
        aliases={0: 0},
    )
    received = lax.ppermute(oth_input, "tensor", swap)

    right, gram, left_rows = call(
        functools.partial(right_kernel, scale),
        [VMEM, VMEM, HBM, HBM, HBM],
        [VMEM, VMEM, HBM],
        [shape((rank, cols), F32), shape((rank, rank), F32), pltpu.HBM((rank, width), BF16)],
        (out_grad, left, acts, acts_oth, error),
        flops=2 * rank * width * 1024,
        moved=17 * MIB,
        scratch=[pltpu.VMEM((tokens + rank, width), BF16), pltpu.VMEM((width, cols), BF16), dma((2 * n_blocks, 3)), dma((1,))],
    )
    rows = exchange(right, 1)
    coeffs, products = call(
        gram_schmidt_kernel, [VMEM], [VMEM] * 2, [shape((rank, rank), F32)] * 2, (gram,), flops=MIB * 1024, moved=8192
    )
    right, right_done = right_sum(rows, coeffs)
    rows = exchange(right, side)
    input_grad, input_done, metric = input_own(0, right_done, gram, coeffs, products)
    right, right_done = right_sum(rows, input_done)
    rows = exchange(right, side * side)
    input_grad, _, first_stack, first_error = input_own(1, right_done, input_grad, acts, acts_oth, error)
    new_error, new_momentum = call(
        functools.partial(final_kernel, scale, 1.0 / replicas),
        [VMEM] * (side + 6) + [HBM] * 3,
        [HBM, VMEM],
        [pltpu.HBM((width, cols), BF16), shape(momentum.shape, BF16)],
        (*rows, metric, out_grad, left_rows, momentum, first_stack, first_error, acts, acts_oth, error),
        flops=2 * (tokens + 3 * rank) * width * cols,
        moved=25 * MIB,
        scratch=[
            pltpu.VMEM((tokens + 3 * rank, width), BF16),
            pltpu.VMEM((tokens + 3 * rank, cols), BF16),
            pltpu.VMEM((width, cols), BF16),
            pltpu.VMEM((4, BLOCK, cols), BF16),
            dma((n_blocks, 3)),
            dma((4,)),
        ],
    )
    return (new_error, new_momentum, input_grad)


def solution(mesh):
    return jax.shard_map(
        per_device,
        mesh=mesh,
        in_specs=(
            P(("dp", "tensor"), None),
            P("dp", "tensor"),
            P(None, "tensor"),
            P("dp", "tensor"),
            P("dp", "tensor"),
            P("tensor", None),
        ),
        out_specs=(P("dp", "tensor"), P("dp", "tensor"), P(("dp", "tensor"), None)),
        check_vma=False,
    )
```
